256 devices in a mesh: axial: 16 (over z, core), cross: 16 (over x, y).
Axes of the slice: x: 4, y: 4, z: 8, core: 2. Of those that a mesh axis runs over, the one named last changes fastest.
Arguments:
- operator_blocks: bfloat16 [16, 16, 64, 8, 64, 64], P('axial', 'cross'), may hold values from -0.00048828125 to 0.00048828125
- prolong_blocks: bfloat16 [16, 16, 64, 64, 256], P('axial', 'cross'), may hold values from -6 to 6
- operator_cols: int32 [16, 16, 64, 8], P('axial', 'cross'), may hold values from 0 to 16383, as said below
- coarse_map: int32 [16384, 4], replicated, may hold values from 0 to 15, as said below
- live_rows: int32 [16, 16], P('axial', 'cross'), may hold values from 32 to 64, as said below
Outputs:
- coarse_matrix: float32 [1024, 1024], replicated
The draws below stay inside these ranges and needn't reach their ends.
Inputs may be any that keep to these rules, and one draw needn't show every extreme that they name: `operator_cols`: A slot of a row in segment s and partition p names a row of partition p in segment s - 1, s or s + 1; slot 0 names the row itself. `coarse_map`: the 4 coarse blocks of one row are distinct, and for a row of segment s they lie among the 5 blocks that begin at min(max(s - 1, 0), 11). `live_rows`: some partition uses all 64 rows in every draw.
All inputs are finite; a program needn't handle non-finite values.
Results may differ from the reference program's by a relative error of at most 0.003.
Values may be sent and summed in bfloat16 or wider, within the bound.
A program may use at most 192 MiB of HBM per device.

```python
import jax
import jax.numpy as jnp
from jax import lax

B = 64
CB = 64
NCB = 16
KA = 8
KP = 4
R = 64
SEGS = 16
PARTS_SIZE = 16
ROWS_ALL = 16384
NC = 1024
KPC = 256
W = 5


def draw_operator_cols(key, part):
    key = jax.random.fold_in(key, 11)
    first_key, second_key = jax.random.split(key)
    shape = (SEGS, PARTS_SIZE, R, KA)
    segment = jnp.arange(SEGS, dtype=jnp.int32)[:, None, None, None]
    section = jnp.arange(PARTS_SIZE, dtype=jnp.int32)[None, :, None, None]
    own_row = jnp.arange(R, dtype=jnp.int32)[None, None, :, None]
    slot = jnp.arange(KA, dtype=jnp.int32)[None, None, None, :]
    offset = jax.random.randint(first_key, shape, -1, 2)
    target_segment = jnp.clip(segment + offset, 0, SEGS - 1)
    target_row = jax.random.randint(second_key, shape, 0, R)
    target_segment = jnp.where(slot == 0, segment, target_segment)
    target_row = jnp.where(slot == 0, own_row, target_row)
    return ((target_segment * PARTS_SIZE + section) * R + target_row).astype(jnp.int32)


def draw_coarse_map(key, part):
    key = jax.random.fold_in(key, 23)
    row_ids = jnp.arange(ROWS_ALL, dtype=jnp.int32)
    segment = row_ids // (PARTS_SIZE * R)
    lowest = jnp.clip(segment * NCB // SEGS - 1, 0, NCB - W)
    scores = jax.random.randint(key, (ROWS_ALL, W), 0, 1048576) * W + jnp.arange(W, dtype=jnp.int32)[None, :]
    order = jnp.argsort(scores, axis=1, stable=True).astype(jnp.int32)
    return (lowest[:, None] + order[:, :KP]).astype(jnp.int32)


def draw_live_rows(key, part):
    key = jax.random.fold_in(key, 37)
    first_key, second_key = jax.random.split(key)
    counts = jax.random.randint(first_key, (SEGS * PARTS_SIZE,), R // 2, R + 1)
    chosen = jax.random.randint(second_key, (), 0, SEGS * PARTS_SIZE)
    counts = jnp.where(jnp.arange(SEGS * PARTS_SIZE, dtype=jnp.int32) == chosen, R, counts)
    return counts.reshape(SEGS, PARTS_SIZE).astype(jnp.int32)


def level_of(own_key, extent, cuts, low, largest):
    def one(axis_at, parts):
        heights = jax.random.uniform(jax.random.fold_in(jax.random.fold_in(own_key, 6), axis_at), (parts,), jnp.float32, low / len(cuts), largest / len(cuts))
        return jnp.repeat(jnp.exp(heights), extent[axis_at] // parts).reshape((-1,) + (1,) * (len(extent) - axis_at - 1))

    factor_of = one(*cuts[0])
    for cut in cuts[1:]:
        factor_of = factor_of * one(*cut)
    return factor_of


def gaussian(stream_key, shape, scale, bound, pieces=(), held_as=jnp.bfloat16):
    values = scale * jax.random.normal(stream_key, shape, jnp.float32)
    if pieces:
        values = values * level_of(stream_key, shape, pieces, -0.22, 0.18)
    return jnp.clip(values, -bound, bound).astype(held_as)


def setup_inputs(seed: int = 0) -> dict:
    arg_keys = jax.random.split(jax.random.key(seed), 6)
    operator_blocks = gaussian(arg_keys[0], (SEGS, PARTS_SIZE, R, KA, B, B), (4 * PARTS_SIZE * R * B * B * KA) ** -0.5, 0.00048828125, ((0, 16), (1, 16)))
    prolong_blocks = gaussian(arg_keys[1], (SEGS, PARTS_SIZE, R, B, KPC), 1.0, 6.0, ((0, 16), (1, 16)))
    operator_cols = draw_operator_cols(jax.random.fold_in(arg_keys[5], 71), 0)
    coarse_map = draw_coarse_map(jax.random.fold_in(arg_keys[5], 71), 0)
    live_rows = draw_live_rows(jax.random.fold_in(arg_keys[5], 71), 0)
    return {"operator_blocks": operator_blocks, "prolong_blocks": prolong_blocks, "operator_cols": operator_cols, "coarse_map": coarse_map, "live_rows": live_rows}


def reference(operator_blocks, prolong_blocks, operator_cols, coarse_map, live_rows):
    alive = jnp.arange(R, dtype=jnp.int32)[None, None, :] < live_rows[:, :, None]
    masked = jnp.where(alive[:, :, :, None, None], prolong_blocks, jnp.zeros((), jnp.bfloat16))
    flat_prolong = masked.reshape(SEGS * PARTS_SIZE * R, B, KP * CB)
    flat_operator = operator_blocks.reshape(SEGS * PARTS_SIZE, R, KA, B, B)
    flat_cols = operator_cols.reshape(SEGS * PARTS_SIZE, R, KA)
    labels = jnp.arange(NCB, dtype=jnp.int32)
    highest = lax.Precision.HIGHEST

    def add_device(accumulated, device):
        columns = flat_cols[device]
        picked = flat_prolong[columns].astype(jnp.float32)
        blocks = flat_operator[device].astype(jnp.float32)
        partial_value = jnp.einsum("rkab,rkbq->rkaq", blocks, picked, precision=highest)
        onehot = (coarse_map[columns][..., None] == labels).astype(jnp.float32)
        spread = jnp.einsum("rkpn,rkapc->ranc", onehot, partial_value.reshape(R, KA, B, KP, CB), precision=highest)
        rounded = lax.optimization_barrier(spread.reshape(R, B, NC).astype(jnp.bfloat16))
        product = rounded.astype(jnp.float32)
        first_row = device * R
        own_rows = lax.dynamic_slice_in_dim(flat_prolong, first_row, R, 0).astype(jnp.float32)
        own_map = lax.dynamic_slice_in_dim(coarse_map, first_row, R, 0)
        own_onehot = (own_map[..., None] == labels).astype(jnp.float32)
        weighted = jnp.einsum("rbq,rbm->rqm", own_rows, product, precision=highest)
        update = jnp.einsum("rpn,rpcm->ncm", own_onehot, weighted.reshape(R, KP, CB, NC), precision=highest)
        return accumulated + update.reshape(NC, NC), None

    result = lax.scan(add_device, jnp.zeros((NC, NC), jnp.float32), jnp.arange(SEGS * PARTS_SIZE, dtype=jnp.int32))[0]
    return result
```

```python
import functools

import jax
import jax.numpy as jnp
from jax import lax
from jax.experimental import pallas as pl
from jax.experimental.pallas import tpu as pltpu
from jax.sharding import PartitionSpec as P

NCB = 16
W = 5
ROWS = 64
MESH = pl.DeviceIdType.MESH
GROUP = 8


def lowest_of(segment):
    return jnp.clip(segment - 1, 0, NCB - W)


def base_of(segment):
    low = lowest_of(jnp.maximum(segment - 1, 0))
    return jnp.minimum(low - low % 2, 8)


def local_kernel(cols, table, own_table, base_half, a_ref, low_ref, own_ref, high_ref, out_ref, tiles, wide, left, product, total):
    step = pl.program_id(0)
    lane_low = lax.broadcasted_iota(jnp.int32, (64, 128), 1) < 64

    @pl.when(step == 0)
    def _():
        tiles[12 * ROWS] = jnp.zeros((64, 128), jnp.bfloat16)
        for part, ref in enumerate((low_ref, own_ref, high_ref)):

            @pl.loop(0, ROWS, unroll=4)
            def _(row, part=part, ref=ref):
                value = ref[row]
                at = 4 * (part * ROWS + row)
                for pair in range(2):
                    tile = value[:, 128 * pair : 128 * pair + 128]
                    tiles[at + pair] = tile
                    tiles[at + 2 + pair] = jnp.concatenate([tile[:, 64:], tile[:, :64]], axis=1)

        @pl.loop(0, 3 * ROWS, unroll=4)
        def _(row):
            for pair in range(4):
                wide[row, :, 128 * pair : 128 * pair + 128] = jnp.where(
                    lane_low, tiles[table[2 * pair, row]], tiles[table[2 * pair + 1, row]]
                )

        total[...] = jnp.zeros_like(total)

    @pl.loop(0, GROUP, unroll=2)
    def _(inner):
        row = step * GROUP + inner
        value = None
        for half in range(2):
            slots = range(4 * half, 4 * half + 4)
            lhs = jnp.concatenate([a_ref[inner, k] for k in slots], axis=1)
            rhs = jnp.concatenate([wide[cols[k, row]] for k in slots], axis=0)
            term = jnp.dot(lhs, rhs, preferred_element_type=jnp.float32)
            value = term if value is None else value + term
        at = pl.ds(pl.multiple_of(inner * 64, 64), 64)
        product[at, :] = value.astype(jnp.bfloat16)
        for pair in range(3):
            left[at, 128 * pair : 128 * pair + 128] = jnp.where(
                lane_low, tiles[own_table[2 * pair, row]], tiles[own_table[2 * pair + 1, row]]
            )

    total[...] += lax.dot_general(
        left[...], product[...], (((0,), (0,)), ((), ())), preferred_element_type=jnp.float32
    )

    @pl.when(step == pl.num_programs(0) - 1)
    def _():
        for quarter in range(4):
            for pair in range(4):
                target = quarter * 4 + lax.rem(base_half[0] + pair, 4)
                for block in range(W):
                    at = block * 64 + quarter * 16
                    out_ref[target, block * 16 : block * 16 + 16, :] = total[
                        at : at + 16, 128 * pair : 128 * pair + 128
                    ].astype(jnp.bfloat16)


def local_part(cols, table, own_table, base_half, blocks, low, own, high):
    smem = pl.BlockSpec(memory_space=pltpu.SMEM)
    whole = pl.BlockSpec((ROWS, 64, 256), lambda i: (0, 0, 0))
    return pl.pallas_call(
        local_kernel,
        grid=(ROWS // GROUP,),
        out_shape=jax.ShapeDtypeStruct((16, 80, 128), jnp.bfloat16),
        in_specs=[
            smem,
            smem,
            smem,
            smem,
            pl.BlockSpec((GROUP, 8, 64, 64), lambda i: (i, 0, 0, 0)),
            whole,
            whole,
            whole,
        ],
        out_specs=pl.BlockSpec((16, 80, 128), lambda i: (0, 0, 0)),
        scratch_shapes=[
            pltpu.VMEM((12 * ROWS + 1, 64, 128), jnp.bfloat16),
            pltpu.VMEM((3 * ROWS, 64, 512), jnp.bfloat16),
            pltpu.VMEM((GROUP * 64, 384), jnp.bfloat16),
            pltpu.VMEM((GROUP * 64, 512), jnp.bfloat16),
            pltpu.VMEM((384, 512), jnp.float32),
        ],
        compiler_params=pltpu.CompilerParams(vmem_limit_bytes=56 * 2**20),
        name="local_part",
    )(cols, table, own_table, base_half, blocks, low, own, high)


def sum_kernel(chunks, gathered, from_cross, from_axial, ready, units, sent, got, sent2, got2, sent3, got3, sent4, got4, sent5, got5):
    seg = lax.axis_index("axial")
    sec = lax.axis_index("cross")
    core = lax.rem(seg, 2)
    layer = seg // 2
    quarter = lax.rem(sec, 4)
    sibling = seg + 1 - 2 * core

    barrier = pltpu.get_barrier_semaphore()
    for d in range(1, 16):
        pl.semaphore_signal(barrier, inc=1, device_id=(seg, lax.rem(sec + d, 16)), device_id_type=MESH)
        pl.semaphore_signal(barrier, inc=1, device_id=(lax.rem(seg + d, 16), sec), device_id_type=MESH)
    pl.semaphore_wait(barrier, 30)

    def cross_copy(d):
        target = lax.rem(sec + d, 16)
        return pltpu.make_async_remote_copy(
            src_ref=chunks.at[target],
            dst_ref=from_cross.at[d],
            send_sem=sent.at[d],
            recv_sem=got.at[d],
            device_id=(seg, target),
            device_id_type=MESH,
        )

    for d in range(1, 16):
        cross_copy(d).start()
    value = chunks[sec].astype(jnp.float32)
    for d in range(1, 16):
        cross_copy(d).wait_recv()
        value = value + from_cross[d].astype(jnp.float32)
    units[0:80, :] = value
    units[80:112, :] = jnp.zeros((32, 128), jnp.float32)

    def half_of(segment):
        start = base_of(segment) // 2
        return (start + lax.rem(quarter - start + 8, 4)) // 4

    my_half = half_of(seg)
    my_low = lowest_of(seg)

    def axial_copy(i):
        block = my_low + i
        owner = (block // 2) * 2 + my_half
        return owner, lax.rem(block, 2), pltpu.make_async_remote_copy(
            src_ref=units.at[pl.ds(16 * i, 16)],
            dst_ref=from_axial.at[seg, lax.rem(block, 2)],
            send_sem=sent2.at[i],
            recv_sem=got2.at[seg, lax.rem(block, 2)],
            device_id=(owner, sec),
            device_id_type=MESH,
        )

    for i in range(W):
        owner, place, copy = axial_copy(i)

        @pl.when(owner != seg)
        def _(copy=copy):
            copy.start()

        @pl.when(owner == seg)
        def _(i=i, place=place):
            from_axial[seg, place] = units[16 * i : 16 * i + 16, :]

    @pl.loop(0, 16)
    def _(source):
        low = lowest_of(source)
        for place in range(2):
            block = 2 * layer + place

            @pl.when((half_of(source) == core) & (block >= low) & (block < low + W))
            def _(place=place):
                @pl.when(source != seg)
                def _():
                    pltpu.make_async_remote_copy(
                        src_ref=units.at[pl.ds(0, 16)],
                        dst_ref=from_axial.at[source, place],
                        send_sem=sent2.at[0],
                        recv_sem=got2.at[source, place],
                        device_id=(sibling, sec),
                        device_id_type=MESH,
                    ).wait_recv()

                units[80 + 16 * place : 96 + 16 * place, :] += from_axial[source, place]

    mine = pl.ds(pl.multiple_of(layer * 32, 32), 32)
    ready[mine, :] = units[80:112, :].astype(jnp.bfloat16)

    def layer_copy(d):
        return pltpu.make_async_remote_copy(
            src_ref=ready.at[mine],
            dst_ref=ready.at[mine],
            send_sem=sent3.at[d],
            recv_sem=got3.at[d],
            device_id=(lax.rem(seg + 2 * d, 16), sec),
            device_id_type=MESH,
        )

    for d in range(1, 8):
        layer_copy(d).start()
    for d in range(1, 8):
        source = pl.ds(pl.multiple_of(lax.rem(layer - d + 8, 8) * 32, 32), 32)
        pltpu.make_async_remote_copy(
            src_ref=ready.at[source],
            dst_ref=ready.at[source],
            send_sem=sent3.at[d],
            recv_sem=got3.at[d],
            device_id=(sibling, sec),
            device_id_type=MESH,
        ).wait_recv()

    first = jnp.where(core == 0, quarter // 3, jnp.minimum(3 + quarter, 4))
    gathered[core, sec] = ready[pl.ds(pl.multiple_of(first * 16, 16), 192), :]

    def share_copy(d):
        return pltpu.make_async_remote_copy(
            src_ref=gathered.at[core, sec],
            dst_ref=gathered.at[core, sec],
            send_sem=sent4.at[d],
            recv_sem=got4.at[d],
            device_id=(seg, lax.rem(sec + d, 16)),
            device_id_type=MESH,
        )

    def pass_copy(half, d):
        section = lax.rem(sec - d + 16, 16)
        return pltpu.make_async_remote_copy(
            src_ref=gathered.at[half, section],
            dst_ref=gathered.at[half, section],
            send_sem=sent5.at[d],
            recv_sem=got5.at[d],
            device_id=(sibling, sec),
            device_id_type=MESH,
        )

    for d in range(1, 16):
        share_copy(d).start()
    pass_copy(core, 0).start()
    for d in range(1, 16):
        section = lax.rem(sec - d + 16, 16)
        pltpu.make_async_remote_copy(
            src_ref=gathered.at[core, section],
            dst_ref=gathered.at[core, section],
            send_sem=sent4.at[d],
            recv_sem=got4.at[d],
            device_id=(sibling, sec),
            device_id_type=MESH,
        ).wait_recv()
        pass_copy(core, d).start()
    for d in range(16):
        pass_copy(1 - core, d).wait_recv()

    for d in range(1, 16):
        cross_copy(d).wait_send()
        share_copy(d).wait_send()
    for d in range(1, 8):
        layer_copy(d).wait_send()
    for d in range(16):
        pass_copy(core, d).wait_send()
    for i in range(W):
        owner, _, copy = axial_copy(i)

        @pl.when(owner != seg)
        def _(copy=copy):
            copy.wait_send()


def sum_over_devices(chunks):
    dma = pltpu.SemaphoreType.DMA
    vmem = pl.BlockSpec(memory_space=pltpu.VMEM)
    return pl.pallas_call(
        sum_kernel,
        out_shape=jax.ShapeDtypeStruct((2, 16, 192, 128), jnp.bfloat16),
        in_specs=[vmem],
        out_specs=vmem,
        scratch_shapes=[
            pltpu.VMEM((16, 80, 128), jnp.bfloat16),
            pltpu.VMEM((16, 2, 16, 128), jnp.float32),
            pltpu.VMEM((256, 128), jnp.bfloat16),
            pltpu.VMEM((112, 128), jnp.float32),
            dma((16,)),
            dma((16,)),
            dma((W,)),
            dma((16, 2)),
            dma((8,)),
            dma((8,)),
            dma((16,)),
            dma((16,)),
            dma((16,)),
            dma((16,)),
        ],
        compiler_params=pltpu.CompilerParams(
            collective_id=0, has_side_effects=True, vmem_limit_bytes=16 * 2**20
        ),
        name="sum_over_devices",
    )(chunks)


def place_kernel(shares, out_ref):
    out_ref[...] = jnp.zeros_like(out_ref)
    for half in range(2):
        for quarter in range(4):
            first = quarter // 3 if half == 0 else min(3 + quarter, 4)
            for part in range(4):
                for unit in range(12):
                    row = (first + unit) * 64 + part * 16
                    column = (quarter + 4 * half) * 128
                    out_ref[row : row + 16, column : column + 128] = shares[
                        half, part * 4 + quarter, unit * 16 : unit * 16 + 16, :
                    ].astype(jnp.float32)


def place(shares):
    vmem = pl.BlockSpec(memory_space=pltpu.VMEM)
    return pl.pallas_call(
        place_kernel,
        out_shape=jax.ShapeDtypeStruct((1024, 1024), jnp.float32),
        in_specs=[vmem],
        out_specs=vmem,
        compiler_params=pltpu.CompilerParams(vmem_limit_bytes=16 * 2**20),
        name="place",
    )(shares)


def tables(operator_cols, coarse_map, live, segment, section):
    base = base_of(segment)
    order = jnp.arange(3 * ROWS, dtype=jnp.int32)
    labels = []
    for offset in (-1, 0, 1):
        near = jnp.clip(segment + offset, 0, 15)
        labels.append(lax.dynamic_slice(coarse_map.T, (0, (near * 16 + section) * ROWS), (4, ROWS)))
    labels = jnp.concatenate(labels, axis=1)
    alive = (order % ROWS) < jnp.repeat(live, ROWS)
    source = jnp.array([[0, 2, 1, 3], [2, 0, 3, 1]], jnp.int32)

    def find(labels, wanted, alive, order):
        hit = labels[None, :, :] == wanted[:, None, None]
        tile = jnp.tile(source, (wanted.shape[0] // 2, 1))[:, :, None]
        found = jnp.sum(jnp.where(hit, 4 * order[None, None, :] + tile, 0), axis=1)
        return jnp.where(jnp.any(hit, axis=1) & alive[None, :], found, 12 * ROWS)

    table = find(labels, base + jnp.arange(8, dtype=jnp.int32), alive, order)
    own = slice(ROWS, 2 * ROWS)
    own_table = find(
        labels[:, own],
        jnp.concatenate([lowest_of(segment) + jnp.arange(W, dtype=jnp.int32), jnp.full((1,), -1, jnp.int32)]),
        alive[own],
        order[own],
    )
    columns = operator_cols[0, 0].T
    columns = (columns // (16 * ROWS) - segment + 1) * ROWS + columns % ROWS
    return columns, table, own_table, jnp.reshape(base // 2, (1,))


def on_device(operator_blocks, prolong_blocks, operator_cols, coarse_map, live_rows):
    segment = lax.axis_index("axial")
    section = lax.axis_index("cross")
    forward = [(i, i + 1) for i in range(15)]
    backward = [(i + 1, i) for i in range(15)]
    own = prolong_blocks[0, 0]
    low = lax.ppermute(own, "axial", forward)
    high = lax.ppermute(own, "axial", backward)
    live = live_rows[0]
    live = jnp.concatenate([lax.ppermute(live, "axial", forward), live, lax.ppermute(live, "axial", backward)])
    columns, table, own_table, base_half = tables(operator_cols, coarse_map, live, segment, section)
    chunks = local_part(columns, table, own_table, base_half, operator_blocks[0, 0], low, own, high)
    return place(sum_over_devices(chunks))


def solution(mesh):
    return jax.shard_map(
        on_device,
        mesh=mesh,
        in_specs=(
            P("axial", "cross", None, None, None, None),
            P("axial", "cross", None, None, None),
            P("axial", "cross", None, None),
            P(),
            P("axial", "cross"),
        ),
        out_specs=P(),
        check_vma=False,
    )
```

```python
import jax
import jax.numpy as jnp
from jax import lax
from jax.experimental import pallas as pl
from jax.experimental.pallas import tpu as pltpu
from jax.sharding import PartitionSpec as P

NCB = 16
W = 5
ROWS = 64
CHUNKS = 4
MESH = pl.DeviceIdType.MESH
EMPTY = 4 * ROWS


def lowest_of(segment):
    return jnp.clip(segment - 1, 0, NCB - W)


def base_of(segment):
    low = lowest_of(jnp.maximum(segment - 1, 0))
    return jnp.minimum(low - low % 2, 8)


def fused_kernel(
    live, cols_ref, map_ref, p_ref, a_ref, gathered,
    maps, tab, own, near, far, blocks, beside, tiles, wide, left, product, total,
    chunks, from_cross, from_axial, ready, units,
    tab_s, load, sent0, got0, sent1, got1, sent2, got2, sent3, got3, sent4, got4, sent5, got5, sent6, got6,
):
    seg = lax.axis_index("axial")
    sec = lax.axis_index("cross")
    core = lax.rem(seg, 2)
    layer = seg // 2
    x = sec // 4
    y = lax.rem(sec, 4)
    sibling = seg + 1 - 2 * core
    beyond = seg - 1 + 2 * core
    has_far = (beyond >= 0) & (beyond < 16)
    beyond = jnp.clip(beyond, 0, 15)
    lane_off = lax.rem(sec, 2) * 64

    def remote(src, dst, send, recv, to):
        return pltpu.make_async_remote_copy(
            src_ref=src, dst_ref=dst, send_sem=send, recv_sem=recv, device_id=to, device_id_type=MESH
        )

    barrier = pltpu.get_barrier_semaphore()
    for d in range(1, 16):
        pl.semaphore_signal(barrier, inc=1, device_id=(lax.rem(seg + d, 16), sec), device_id_type=MESH)
        pl.semaphore_signal(barrier, inc=1, device_id=(seg, lax.rem(sec + d, 16)), device_id_type=MESH)

    step = ROWS // CHUNKS
    own_loads = []
    for c in range(CHUNKS):
        rows = pl.ds(step * c, step)
        own_loads.append(pltpu.make_async_copy(p_ref.at[rows], own.at[rows], load.at[c]))
        own_loads[c].start()
    map_loads = []
    for part, near_seg in enumerate((seg, sibling, beyond)):
        start = pl.multiple_of((near_seg * 16 + sec - lax.rem(sec, 2)) * ROWS, 128)
        map_loads.append(pltpu.make_async_copy(map_ref.at[:, pl.ds(start, 128)], maps.at[part], load.at[CHUNKS + part]))
        map_loads[part].start()
    block_loads = []
    for c in range(2):
        rows = pl.ds(32 * c, 32)
        block_loads.append(pltpu.make_async_copy(a_ref.at[rows], blocks.at[rows], load.at[CHUNKS + 3 + c]))
        block_loads[c].start()

    def near_copy(c):
        rows = pl.ds(step * c, step)
        return remote(own.at[rows], near.at[rows], sent0.at[0, c], got0.at[0, c], (sibling, sec))

    def far_copy(c):
        rows = pl.ds(step * c, step)
        return remote(own.at[rows], far.at[rows], sent0.at[1, c], got0.at[1, c], (beyond, sec))

    in_use = live[0, 0]
    for c in range(CHUNKS):
        own_loads[c].wait()

        @pl.loop(step * c, step * c + step, unroll=4)
        def _(row):
            own[row] = jnp.where(row < in_use, own[row], jnp.zeros((64, 256), jnp.bfloat16))

        if c == 0:
            pl.semaphore_wait(barrier, 30)

        @pl.when(has_far)
        def _(c=c):
            far_copy(c).start()

    for c in range(CHUNKS):
        near_copy(c).start()

    slot = lax.broadcasted_iota(jnp.int32, (8, 128), 0)
    local = lax.broadcasted_iota(jnp.int32, (8, 128), 1) - lane_off
    odd = lax.rem(slot, 2)

    def find(labels, first):
        found = jnp.full((8, 128), EMPTY, jnp.int32)
        for b in range(4):
            even_tile, odd_tile = (0, 2, 1, 3)[b], (2, 0, 3, 1)[b]
            tile = even_tile + odd * (odd_tile - even_tile)
            found = jnp.where(labels[b : b + 1, :] - first == slot, 4 * local + tile, found)
        return found

    base = base_of(seg)
    for part in range(3):
        map_loads[part].wait()
        labels = maps[part]
        tab[part] = find(labels, base)
        if part == 0:
            tab[3] = find(labels, lowest_of(seg))
    named = cols_ref[...]
    named_seg = lax.shift_right_logical(named, 10)
    part = jnp.where(named_seg == seg, 0, jnp.where(named_seg == sibling, 1, 2))
    tab[4, :, 0:64] = part * ROWS + (named & 63)
    tab[4, :, 64:128] = jnp.zeros((8, 64), jnp.int32)
    to_smem = pltpu.make_async_copy(tab, tab_s, load.at[CHUNKS + 5])
    to_smem.start()

    lane_low = lax.broadcasted_iota(jnp.int32, (64, 128), 1) < 64
    tiles[EMPTY] = jnp.zeros((64, 128), jnp.bfloat16)

    def half_tiles(which, row, pair):
        return jnp.where(
            lane_low,
            tiles[tab_s[which, 2 * pair, lane_off + row]],
            tiles[tab_s[which, 2 * pair + 1, lane_off + row]],
        )

    def store_tiles(source, first, count):
        @pl.loop(first, first + count, unroll=4)
        def _(row):
            value = source[row]
            for pair in range(2):
                tile = value[:, 128 * pair : 128 * pair + 128]
                tiles[4 * row + pair] = tile
                tiles[4 * row + 2 + pair] = jnp.concatenate([tile[:, 64:], tile[:, :64]], axis=1)

    def widen(part, first, count):
        @pl.loop(first, first + count, unroll=4)
        def _(row):
            for pair in range(4):
                wide[part * ROWS + row, :, 128 * pair : 128 * pair + 128] = half_tiles(part, row, pair)

    store_tiles(own, 0, ROWS)
    to_smem.wait()
    widen(0, 0, ROWS)

    @pl.loop(0, ROWS, unroll=4)
    def _(row):
        for pair in range(3):
            left[pl.ds(pl.multiple_of(row * 64, 64), 64), 128 * pair : 128 * pair + 128] = half_tiles(3, row, pair)

    for c in range(2):
        block_loads[c].wait()

        @pl.loop(32 * c, 32 * c + 32, unroll=2)
        def _(row):
            for pair in range(4):
                beside[row, :, 128 * pair : 128 * pair + 128] = jnp.concatenate(
                    [blocks[row, 2 * pair], blocks[row, 2 * pair + 1]], axis=1
                )

    for c in range(CHUNKS):
        near_copy(c).wait_recv()
    store_tiles(near, 0, ROWS)
    widen(1, 0, ROWS)

    for c in range(CHUNKS):

        @pl.when(has_far)
        def _(c=c):
            far_copy(c).wait_recv()
            store_tiles(far, step * c, step)
            widen(2, step * c, step)

    @pl.loop(0, ROWS, unroll=2)
    def _(row):
        value = None
        for half in range(2):
            rhs = jnp.concatenate([wide[tab_s[4, k, row]] for k in range(4 * half, 4 * half + 4)], axis=0)
            term = jnp.dot(
                beside[row, :, 256 * half : 256 * half + 256], rhs, preferred_element_type=jnp.float32
            )
            value = term if value is None else value + term
        product[pl.ds(pl.multiple_of(row * 64, 64), 64), :] = value.astype(jnp.bfloat16)

    def cross_send(target):
        return remote(chunks.at[target], from_cross.at[sec], sent1.at[target], got1.at[sec], (seg, target))

    for half in range(2):
        columns = slice(256 * half, 256 * half + 256)
        total[...] = jnp.zeros_like(total)

        @pl.loop(0, 8)
        def _(group, columns=columns):
            rows = pl.ds(pl.multiple_of(group * 512, 512), 512)
            total[...] += lax.dot_general(
                left[rows, :], product[rows, columns], (((0,), (0,)), ((), ())), preferred_element_type=jnp.float32
            )

        for quarter in range(4):
            for pair in range(2):
                target = quarter * 4 + lax.rem(base // 2 + 2 * half + pair, 4)
                for block in range(W):
                    at = block * 64 + quarter * 16
                    chunks[target, block * 16 : block * 16 + 16, :] = total[
                        at : at + 16, 128 * pair : 128 * pair + 128
                    ].astype(jnp.bfloat16)

                @pl.when(target != sec)
                def _(target=target):
                    cross_send(target).start()

    value = chunks[sec].astype(jnp.float32)
    for d in range(1, 16):
        source = lax.rem(sec + d, 16)
        remote(chunks.at[source], from_cross.at[source], sent1.at[source], got1.at[source], (seg, source)).wait_recv()
        value = value + from_cross[source].astype(jnp.float32)
    units[0:80, :] = value
    units[80:112, :] = jnp.zeros((32, 128), jnp.float32)

    def half_of(segment):
        start = base_of(segment) // 2
        return (start + lax.rem(y - start + 8, 4)) // 4

    my_half = half_of(seg)
    my_low = lowest_of(seg)

    def axial_copy(i):
        block = my_low + i
        owner = (block // 2) * 2 + my_half
        place = lax.rem(block, 2)
        copy = remote(
            units.at[pl.ds(16 * i, 16)], from_axial.at[seg, place], sent2.at[i], got2.at[seg, place], (owner, sec)
        )
        return owner, place, copy

    for i in range(W):
        owner, place, copy = axial_copy(i)

        @pl.when(owner != seg)
        def _(copy=copy):
            copy.start()

        @pl.when(owner == seg)
        def _(i=i, place=place):
            from_axial[seg, place] = units[16 * i : 16 * i + 16, :]

    @pl.loop(0, 16)
    def _(source):
        low = lowest_of(source)
        for place in range(2):
            block = 2 * layer + place

            @pl.when((half_of(source) == core) & (block >= low) & (block < low + W))
            def _(place=place):
                @pl.when(source != seg)
                def _():
                    remote(
                        units.at[pl.ds(0, 16)],
                        from_axial.at[source, place],
                        sent2.at[0],
                        got2.at[source, place],
                        (sibling, sec),
                    ).wait_recv()

                units[80 + 16 * place : 96 + 16 * place, :] += from_axial[source, place]

    mine = pl.ds(pl.multiple_of(layer * 32, 32), 32)
    ready[mine, :] = units[80:112, :].astype(jnp.bfloat16)

    def layer_copy(d):
        return remote(ready.at[mine], ready.at[mine], sent3.at[d], got3.at[d], (lax.rem(seg + 2 * d, 16), sec))

    for d in range(1, 8):
        layer_copy(d).start()
    for d in range(1, 8):
        source = pl.ds(pl.multiple_of(lax.rem(layer - d + 8, 8) * 32, 32), 32)
        remote(ready.at[source], ready.at[source], sent3.at[d], got3.at[d], (sibling, sec)).wait_recv()

    first = jnp.where(core == 0, y // 3, jnp.minimum(3 + y, 4))
    gathered[core, 0, y, x] = ready[pl.ds(pl.multiple_of(first * 16, 16), 96), :]
    gathered[core, 1, x, y] = ready[pl.ds(pl.multiple_of(first * 16 + 96, 16), 96), :]

    def moved(which, d):
        return (seg, lax.rem(x + d, 4) * 4 + y) if which == 0 else (seg, x * 4 + lax.rem(y + d, 4))

    def back(which, d):
        return lax.rem((x if which == 0 else y) - d + 4, 4)

    def one_copy(which, d):
        major, minor = (y, x) if which == 0 else (x, y)
        share = gathered.at[core, which, major, minor]
        return remote(share, share, sent4.at[which, d], got4.at[which, d], moved(which, d))

    def four_copy(which, d):
        shares = gathered.at[core, which, y if which == 0 else x]
        return remote(shares, shares, sent5.at[which, d], got5.at[which, d], moved(1 - which, d))

    def pass_copy(half, which, d):
        shares = gathered.at[half, which, back(1 - which, d)]
        return remote(shares, shares, sent6.at[which, d], got6.at[which, d], (sibling, sec))

    for d in (2, 1, 3):
        for which in range(2):
            one_copy(which, d).start()
    for which in range(2):
        for d in (1, 3, 2):
            share = gathered.at[core, which, y if which == 0 else x, back(which, d)]
            remote(share, share, sent4.at[which, d], got4.at[which, d], (sibling, sec)).wait_recv()
        for d in (2, 1, 3):
            four_copy(which, d).start()
    for which in range(2):
        pass_copy(core, which, 0).start()
    for d in (1, 3, 2):
        for which in range(2):
            shares = gathered.at[core, which, back(1 - which, d)]
            remote(shares, shares, sent5.at[which, d], got5.at[which, d], (sibling, sec)).wait_recv()
            pass_copy(core, which, d).start()
    for which in range(2):
        for d in range(4):
            pass_copy(1 - core, which, d).wait_recv()

    for c in range(CHUNKS):
        near_copy(c).wait_send()

        @pl.when(has_far)
        def _(c=c):
            far_copy(c).wait_send()

    for d in range(1, 16):
        cross_send(lax.rem(sec + d, 16)).wait_send()
    for i in range(W):
        owner, _, copy = axial_copy(i)

        @pl.when(owner != seg)
        def _(copy=copy):
            copy.wait_send()

    for d in range(1, 8):
        layer_copy(d).wait_send()
    for which in range(2):
        for d in range(1, 4):
            one_copy(which, d).wait_send()
            four_copy(which, d).wait_send()
        for d in range(4):
            pass_copy(core, which, d).wait_send()


def fused(live, cols, coarse, prolong, operator):
    dma = pltpu.SemaphoreType.DMA
    vmem = pl.BlockSpec(memory_space=pltpu.VMEM)
    anywhere = pl.BlockSpec(memory_space=pl.ANY)
    bf16, f32, i32 = jnp.bfloat16, jnp.float32, jnp.int32
    return pl.pallas_call(
        fused_kernel,
        out_shape=jax.ShapeDtypeStruct((2, 2, 4, 4, 96, 128), bf16),
        in_specs=[pl.BlockSpec(memory_space=pltpu.SMEM), vmem, anywhere, anywhere, anywhere],
        out_specs=vmem,
        scratch_shapes=[
            pltpu.VMEM((3, 4, 128), i32),
            pltpu.VMEM((5, 8, 128), i32),
            pltpu.VMEM((ROWS, 64, 256), bf16),
            pltpu.VMEM((ROWS, 64, 256), bf16),
            pltpu.VMEM((ROWS, 64, 256), bf16),
            pltpu.VMEM((ROWS, 8, 64, 64), bf16),
            pltpu.VMEM((ROWS, 64, 512), bf16),
            pltpu.VMEM((4 * ROWS + 1, 64, 128), bf16),
            pltpu.VMEM((3 * ROWS, 64, 512), bf16),
            pltpu.VMEM((ROWS * 64, 384), bf16),
            pltpu.VMEM((ROWS * 64, 512), bf16),
            pltpu.VMEM((384, 256), f32),
            pltpu.VMEM((16, 80, 128), bf16),
            pltpu.VMEM((16, 80, 128), bf16),
            pltpu.VMEM((16, 2, 16, 128), f32),
            pltpu.VMEM((256, 128), bf16),
            pltpu.VMEM((112, 128), f32),
            pltpu.SMEM((5, 8, 128), i32),
            dma((CHUNKS + 6,)),
            dma((2, CHUNKS)),
            dma((2, CHUNKS)),
            dma((16,)),
            dma((16,)),
            dma((W,)),
            dma((16, 2)),
            dma((8,)),
            dma((8,)),
            dma((2, 4)),
            dma((2, 4)),
            dma((2, 4)),
            dma((2, 4)),
            dma((2, 4)),
            dma((2, 4)),
        ],
        compiler_params=pltpu.CompilerParams(collective_id=0, has_side_effects=True, vmem_limit_bytes=58 * 2**20),
        name="fused",
    )(live, cols, coarse, prolong, operator)


def place_kernel(shares, out_ref):
    out_ref[...] = jnp.zeros_like(out_ref)
    for half in range(2):
        for y in range(4):
            first = y // 3 if half == 0 else min(3 + y, 4)
            for x in range(4):
                for unit in range(12):
                    row = (first + unit) * 64 + x * 16
                    column = (y + 4 * half) * 128
                    at = (half, 0, y, x) if unit < 6 else (half, 1, x, y)
                    out_ref[row : row + 16, column : column + 128] = shares[
                        (*at, slice(unit % 6 * 16, unit % 6 * 16 + 16), slice(None))
                    ].astype(jnp.float32)


def place(shares):
    vmem = pl.BlockSpec(memory_space=pltpu.VMEM)
    return pl.pallas_call(
        place_kernel,
        out_shape=jax.ShapeDtypeStruct((1024, 1024), jnp.float32),
        in_specs=[vmem],
        out_specs=vmem,
        compiler_params=pltpu.CompilerParams(vmem_limit_bytes=16 * 2**20),
        name="place",
    )(shares)


def on_device(operator_blocks, prolong_blocks, operator_cols, coarse_map, live_rows):
    shares = fused(live_rows, operator_cols[0, 0].T, coarse_map.T, prolong_blocks[0, 0], operator_blocks[0, 0])
    return place(shares)


def solution(mesh):
    return jax.shard_map(
        on_device,
        mesh=mesh,
        in_specs=(
            P("axial", "cross", None, None, None, None),
            P("axial", "cross", None, None, None),
            P("axial", "cross", None, None),
            P(),
            P("axial", "cross"),
        ),
        out_specs=P(),
        check_vma=False,
    )
```

```python
import jax
import jax.numpy as jnp
from jax import lax
from jax.experimental import pallas as pl
from jax.experimental.pallas import tpu as pltpu
from jax.sharding import PartitionSpec as P

NCB = 16
W = 5
ROWS = 64
PIECES = ((0, 32), (32, 48), (48, 64))
CHUNKS = len(PIECES)
MESH = pl.DeviceIdType.MESH
EMPTY = 4 * ROWS


def lowest_of(segment):
    return jnp.clip(segment - 1, 0, NCB - W)


def base_of(segment):
    low = lowest_of(jnp.maximum(segment - 1, 0))
    return jnp.minimum(low - low % 2, 8)


def fused_kernel(
    live, cols_ref, map_ref, p_ref, a_ref, shares_out,
    maps, tab, own, near, far, blocks, beside, tiles, wide, left, turned, partial, product, total, gathered,
    chunks, from_cross, from_axial, ready, units,
    tab_s, load, sent0, got0, sent1, got1, sent2, got2, sent3, got3, sent4, got4, sent5, got5, sent6, got6, flush,
):
    seg = lax.axis_index("axial")
    sec = lax.axis_index("cross")
    core = lax.rem(seg, 2)
    layer = seg // 2
    x = sec // 4
    y = lax.rem(sec, 4)
    sibling = seg + 1 - 2 * core
    beyond = seg - 1 + 2 * core
    has_far = (beyond >= 0) & (beyond < 16)
    beyond = jnp.clip(beyond, 0, 15)
    lane_off = lax.rem(sec, 2) * 64

    def remote(src, dst, send, recv, to):
        return pltpu.make_async_remote_copy(
            src_ref=src, dst_ref=dst, send_sem=send, recv_sem=recv, device_id=to, device_id_type=MESH
        )

    barrier = pltpu.get_barrier_semaphore()
    for d in range(1, 16):
        pl.semaphore_signal(barrier, inc=1, device_id=(lax.rem(seg + d, 16), sec), device_id_type=MESH)
        pl.semaphore_signal(barrier, inc=1, device_id=(seg, lax.rem(sec + d, 16)), device_id_type=MESH)

    def piece(ref, c):
        return ref.at[:, pl.ds(PIECES[c][0], PIECES[c][1] - PIECES[c][0]), :]

    own_loads = [pltpu.make_async_copy(piece(p_ref, c), piece(own, c), load.at[c]) for c in range(CHUNKS)]
    for copy in own_loads:
        copy.start()
    map_loads = []
    for part, near_seg in enumerate((seg, sibling, beyond)):
        start = pl.multiple_of((near_seg * 16 + sec - lax.rem(sec, 2)) * ROWS, 128)
        map_loads.append(pltpu.make_async_copy(map_ref.at[:, pl.ds(start, 128)], maps.at[part], load.at[CHUNKS + part]))
        map_loads[part].start()

    def block_load(c):
        return pltpu.make_async_copy(a_ref.at[pl.ds(16 * c, 16)], blocks.at[c % 2], load.at[CHUNKS + 3 + c])

    for c in range(2):
        block_load(c).start()

    def near_copy():
        return remote(own, near, sent0.at[CHUNKS], got0.at[CHUNKS], (sibling, sec))

    def far_copy(c):
        return remote(piece(own, c), piece(far, c), sent0.at[c], got0.at[c], (beyond, sec))

    in_use = live[0, 0]
    for c, (lo, hi) in enumerate(PIECES):
        own_loads[c].wait()

        @pl.loop(0, ROWS, unroll=8)
        def _(row, lo=lo, hi=hi):
            own[row, lo:hi, :] = jnp.where(row < in_use, own[row, lo:hi, :], jnp.zeros((hi - lo, 256), jnp.bfloat16))

        if c == 0:
            pl.semaphore_wait(barrier, 30)

        @pl.when(has_far)
        def _(c=c):
            far_copy(c).start()

    near_copy().start()

    slot = lax.broadcasted_iota(jnp.int32, (8, 128), 0)
    local = lax.broadcasted_iota(jnp.int32, (8, 128), 1) - lane_off
    odd = lax.rem(slot, 2)

    def find(labels, first):
        found = jnp.full((8, 128), EMPTY, jnp.int32)
        for b in range(4):
            even_tile, odd_tile = (0, 2, 1, 3)[b], (2, 0, 3, 1)[b]
            tile = even_tile + odd * (odd_tile - even_tile)
            found = jnp.where(labels[b : b + 1, :] - first == slot, 4 * local + tile, found)
        return found

    base = base_of(seg)
    for part in range(3):
        map_loads[part].wait()
        labels = maps[part]
        tab[part] = find(labels, base)
        if part == 0:
            tab[3] = find(labels, lowest_of(seg))
    named = cols_ref[...]
    named_seg = lax.shift_right_logical(named, 10)
    part = jnp.where(named_seg == seg, 0, jnp.where(named_seg == sibling, 1, 2))
    tab[4, :, 0:64] = part * ROWS + (named & 63)
    tab[4, :, 64:128] = jnp.zeros((8, 64), jnp.int32)
    to_smem = pltpu.make_async_copy(tab, tab_s, load.at[CHUNKS + 7])
    to_smem.start()

    lane_low = lax.broadcasted_iota(jnp.int32, (64, 128), 1) < 64
    tiles[EMPTY] = jnp.zeros((64, 128), jnp.bfloat16)

    def half_tiles(which, row, pair, lo, hi):
        return jnp.where(
            lane_low[lo:hi, :],
            tiles[tab_s[which, 2 * pair, lane_off + row], lo:hi, :],
            tiles[tab_s[which, 2 * pair + 1, lane_off + row], lo:hi, :],
        )

    def store_tiles(source, lo, hi):
        @pl.loop(0, ROWS, unroll=4)
        def _(row):
            value = source[row, lo:hi, :]
            for pair in range(2):
                tile = value[:, 128 * pair : 128 * pair + 128]
                tiles[4 * row + pair, lo:hi, :] = tile
                tiles[4 * row + 2 + pair, lo:hi, :] = jnp.concatenate([tile[:, 64:], tile[:, :64]], axis=1)

    def widen(part, lo, hi):
        @pl.loop(0, ROWS, unroll=4)
        def _(row):
            for pair in range(4):
                wide[part * ROWS + row, lo:hi, 128 * pair : 128 * pair + 128] = half_tiles(part, row, pair, lo, hi)

    store_tiles(own, 0, 64)
    to_smem.wait()
    widen(0, 0, 64)

    @pl.loop(0, 8)
    def _(group):
        for inner in range(8):
            for pair in range(3):
                left[64 * inner : 64 * inner + 64, 128 * pair : 128 * pair + 128] = half_tiles(
                    3, group * 8 + inner, pair, 0, 64
                )
        turned[group] = left[...].T

    for c in range(4):
        block_load(c).wait()

        @pl.loop(0, 16, unroll=2)
        def _(row, c=c):
            at = 0
            for lo, hi in PIECES:
                width = 8 * (hi - lo)
                beside[16 * c + row, :, at : at + width] = jnp.concatenate(
                    [blocks[c % 2, row, k][:, lo:hi] for k in range(8)], axis=1
                )
                at += width

        if c < 2:
            block_load(c + 2).start()

    near_copy().wait_recv()
    store_tiles(near, 0, 64)
    widen(1, 0, 64)

    for c, (lo, hi) in enumerate(PIECES):

        @pl.when(has_far)
        def _(c=c, lo=lo, hi=hi):
            far_copy(c).wait_recv()
            store_tiles(far, lo, hi)
            widen(2, lo, hi)

        @pl.loop(0, ROWS, unroll=4)
        def _(row, c=c, lo=lo, hi=hi):
            rhs = jnp.concatenate([wide[tab_s[4, k, row], lo:hi, :] for k in range(8)], axis=0)
            term = jnp.dot(beside[row, :, 8 * lo : 8 * hi], rhs, preferred_element_type=jnp.float32)
            at = pl.ds(pl.multiple_of(row * 64, 64), 64)
            if c > 0:
                term = partial[at, :] + term
            if c < CHUNKS - 1:
                partial[at, :] = term
            else:
                product[at, :] = term.astype(jnp.bfloat16)

    def cross_send(target):
        return remote(chunks.at[target], from_cross.at[sec], sent1.at[target], got1.at[sec], (seg, target))

    for half in range(2):
        columns = slice(256 * half, 256 * half + 256)
        value = None
        for group in range(8):
            term = jnp.dot(
                turned[group], product[512 * group : 512 * group + 512, columns], preferred_element_type=jnp.float32
            )
            value = term if value is None else value + term
        total[...] = value

        for quarter in range(4):
            for pair in range(2):
                target = quarter * 4 + lax.rem(base // 2 + 2 * half + pair, 4)
                for block in range(W):
                    at = block * 64 + quarter * 16
                    chunks[target, block * 16 : block * 16 + 16, :] = total[
                        at : at + 16, 128 * pair : 128 * pair + 128
                    ].astype(jnp.bfloat16)

                @pl.when(target != sec)
                def _(target=target):
                    cross_send(target).start()

    value = chunks[sec].astype(jnp.float32)
    for d in range(1, 16):
        source = lax.rem(sec + d, 16)
        remote(chunks.at[source], from_cross.at[source], sent1.at[source], got1.at[source], (seg, source)).wait_recv()
        value = value + from_cross[source].astype(jnp.float32)
    units[0:80, :] = value
    units[80:112, :] = jnp.zeros((32, 128), jnp.float32)

    def half_of(segment):
        start = base_of(segment) // 2
        return (start + lax.rem(y - start + 8, 4)) // 4

    my_half = half_of(seg)
    my_low = lowest_of(seg)

    def axial_copy(i):
        block = my_low + i
        owner = (block // 2) * 2 + my_half
        place = lax.rem(block, 2)
        copy = remote(
            units.at[pl.ds(16 * i, 16)], from_axial.at[seg, place], sent2.at[i], got2.at[seg, place], (owner, sec)
        )
        return owner, place, copy

    for i in range(W):
        owner, place, copy = axial_copy(i)

        @pl.when(owner != seg)
        def _(copy=copy):
            copy.start()

        @pl.when(owner == seg)
        def _(i=i, place=place):
            from_axial[seg, place] = units[16 * i : 16 * i + 16, :]

    @pl.loop(0, 16)
    def _(source):
        low = lowest_of(source)
        for place in range(2):
            block = 2 * layer + place

            @pl.when((half_of(source) == core) & (block >= low) & (block < low + W))
            def _(place=place):
                @pl.when(source != seg)
                def _():
                    remote(
                        units.at[pl.ds(0, 16)],
                        from_axial.at[source, place],
                        sent2.at[0],
                        got2.at[source, place],
                        (sibling, sec),
                    ).wait_recv()

                units[80 + 16 * place : 96 + 16 * place, :] += from_axial[source, place]

    mine = pl.ds(pl.multiple_of(layer * 32, 32), 32)
    ready[mine, :] = units[80:112, :].astype(jnp.bfloat16)

    def layer_copy(d):
        return remote(ready.at[mine], ready.at[mine], sent3.at[d], got3.at[d], (lax.rem(seg + 2 * d, 16), sec))

    for d in range(1, 8):
        layer_copy(d).start()
    for d in range(1, 8):
        source = pl.ds(pl.multiple_of(lax.rem(layer - d + 8, 8) * 32, 32), 32)
        remote(ready.at[source], ready.at[source], sent3.at[d], got3.at[d], (sibling, sec)).wait_recv()

    first = jnp.where(core == 0, y // 3, jnp.minimum(3 + y, 4))
    gathered[0, y, x] = ready[pl.ds(pl.multiple_of(first * 16, 16), 96), :]
    gathered[1, x, y] = ready[pl.ds(pl.multiple_of(first * 16 + 96, 16), 96), :]

    def moved(which, d):
        return (seg, lax.rem(x + d, 4) * 4 + y) if which == 0 else (seg, x * 4 + lax.rem(y + d, 4))

    def back(which, d):
        return lax.rem((x if which == 0 else y) - d + 4, 4)

    def one_copy(which, d):
        major, minor = (y, x) if which == 0 else (x, y)
        share = gathered.at[which, major, minor]
        return remote(share, share, sent4.at[which, d], got4.at[which, d], moved(which, d))

    def four_copy(which, d):
        shares = gathered.at[which, y if which == 0 else x]
        return remote(shares, shares, sent5.at[which, d], got5.at[which, d], moved(1 - which, d))

    def pass_copy(half, which, d):
        place = back(1 - which, d)
        shares = gathered.at[which, place]
        return remote(shares, shares_out.at[half, which, place], sent6.at[which, d], got6.at[which, d], (sibling, sec))

    def keep_copy(which, d):
        place = back(1 - which, d)
        return pltpu.make_async_copy(gathered.at[which, place], shares_out.at[core, which, place], flush.at[which, d])

    for d in (2, 1, 3):
        for which in range(2):
            one_copy(which, d).start()
    for which in range(2):
        for d in (1, 3, 2):
            share = gathered.at[which, y if which == 0 else x, back(which, d)]
            remote(share, share, sent4.at[which, d], got4.at[which, d], (sibling, sec)).wait_recv()
        for d in (2, 1, 3):
            four_copy(which, d).start()
    for which in range(2):
        pass_copy(core, which, 0).start()
        keep_copy(which, 0).start()
    for d in (1, 3, 2):
        for which in range(2):
            shares = gathered.at[which, back(1 - which, d)]
            remote(shares, shares, sent5.at[which, d], got5.at[which, d], (sibling, sec)).wait_recv()
            pass_copy(core, which, d).start()
            keep_copy(which, d).start()
    for which in range(2):
        for d in range(4):
            pass_copy(1 - core, which, d).wait_recv()

    near_copy().wait_send()
    for c in range(CHUNKS):

        @pl.when(has_far)
        def _(c=c):
            far_copy(c).wait_send()

    for d in range(1, 16):
        cross_send(lax.rem(sec + d, 16)).wait_send()
    for i in range(W):
        owner, _, copy = axial_copy(i)

        @pl.when(owner != seg)
        def _(copy=copy):
            copy.wait_send()

    for d in range(1, 8):
        layer_copy(d).wait_send()
    for which in range(2):
        for d in range(1, 4):
            one_copy(which, d).wait_send()
            four_copy(which, d).wait_send()
        for d in range(4):
            pass_copy(core, which, d).wait_send()
            keep_copy(which, d).wait()


def fused(live, cols, coarse, prolong, operator):
    dma = pltpu.SemaphoreType.DMA
    vmem = pl.BlockSpec(memory_space=pltpu.VMEM)
    anywhere = pl.BlockSpec(memory_space=pl.ANY)
    bf16, f32, i32 = jnp.bfloat16, jnp.float32, jnp.int32
    return pl.pallas_call(
        fused_kernel,
        out_shape=jax.ShapeDtypeStruct((2, 2, 4, 4, 96, 128), bf16),
        in_specs=[pl.BlockSpec(memory_space=pltpu.SMEM), vmem, anywhere, anywhere, anywhere],
        out_specs=anywhere,
        scratch_shapes=[
            pltpu.VMEM((3, 4, 128), i32),
            pltpu.VMEM((5, 8, 128), i32),
            pltpu.VMEM((ROWS, 64, 256), bf16),
            pltpu.VMEM((ROWS, 64, 256), bf16),
            pltpu.VMEM((ROWS, 64, 256), bf16),
            pltpu.VMEM((2, 16, 8, 64, 64), bf16),
            pltpu.VMEM((ROWS, 64, 512), bf16),
            pltpu.VMEM((4 * ROWS + 1, 64, 128), bf16),
            pltpu.VMEM((3 * ROWS, 64, 512), bf16),
            pltpu.VMEM((512, 384), bf16),
            pltpu.VMEM((8, 384, 512), bf16),
            pltpu.VMEM((ROWS * 64, 512), f32),
            pltpu.VMEM((ROWS * 64, 512), bf16),
            pltpu.VMEM((384, 256), f32),
            pltpu.VMEM((2, 4, 4, 96, 128), bf16),
            pltpu.VMEM((16, 80, 128), bf16),
            pltpu.VMEM((16, 80, 128), bf16),
            pltpu.VMEM((16, 2, 16, 128), f32),
            pltpu.VMEM((256, 128), bf16),
            pltpu.VMEM((112, 128), f32),
            pltpu.SMEM((5, 8, 128), i32),
            dma((CHUNKS + 8,)),
            dma((CHUNKS + 1,)),
            dma((CHUNKS + 1,)),
            dma((16,)),
            dma((16,)),
            dma((W,)),
            dma((16, 2)),
            dma((8,)),
            dma((8,)),
            dma((2, 4)),
            dma((2, 4)),
            dma((2, 4)),
            dma((2, 4)),
            dma((2, 4)),
            dma((2, 4)),
            dma((2, 4)),
        ],
        compiler_params=pltpu.CompilerParams(collective_id=0, has_side_effects=True, vmem_limit_bytes=61 * 2**20),
        name="fused",
    )(live, cols, coarse, prolong, operator)


def place_kernel(first_share, second_share, out_ref):
    half, low_y = pl.program_id(0) // 2, lax.rem(pl.program_id(0), 2) * 2
    out_ref[...] = jnp.zeros_like(out_ref)
    for j in range(2):
        y = low_y + j
        first = jnp.where(half == 0, y // 3, jnp.minimum(3 + y, 4))
        for x in range(4):
            for unit in range(12):
                row = pl.multiple_of((first + unit) * 64 + x * 16, 16)
                rows = slice(unit % 6 * 16, unit % 6 * 16 + 16)
                value = first_share[0, 0, j, x, rows, :] if unit < 6 else second_share[0, 0, x, j, rows, :]
                out_ref[pl.ds(row, 16), 128 * j : 128 * j + 128] = value.astype(jnp.float32)


def place(shares):
    return pl.pallas_call(
        place_kernel,
        grid=(4,),
        out_shape=jax.ShapeDtypeStruct((1024, 1024), jnp.float32),
        in_specs=[
            pl.BlockSpec((1, 1, 2, 4, 96, 128), lambda i: (i // 2, 0, i % 2, 0, 0, 0)),
            pl.BlockSpec((1, 1, 4, 2, 96, 128), lambda i: (i // 2, 1, 0, i % 2, 0, 0)),
        ],
        out_specs=pl.BlockSpec((1024, 256), lambda i: (0, i)),
        compiler_params=pltpu.CompilerParams(vmem_limit_bytes=16 * 2**20),
        name="place",
    )(shares, shares)


def on_device(operator_blocks, prolong_blocks, operator_cols, coarse_map, live_rows):
    shares = fused(live_rows, operator_cols[0, 0].T, coarse_map.T, prolong_blocks[0, 0], operator_blocks[0, 0])
    return place(shares)


def solution(mesh):
    return jax.shard_map(
        on_device,
        mesh=mesh,
        in_specs=(
            P("axial", "cross", None, None, None, None),
            P("axial", "cross", None, None, None),
            P("axial", "cross", None, None),
            P(),
            P("axial", "cross"),
        ),
        out_specs=P(),
        check_vma=False,
    )
```

```python
import jax
import jax.numpy as jnp
from jax import lax
from jax.experimental import pallas as pl
from jax.experimental.pallas import tpu as pltpu
from jax.sharding import PartitionSpec as P

NCB = 16
W = 5
ROWS = 64
PIECES = ((0, 32), (32, 64))
CHUNKS = len(PIECES)
MESH = pl.DeviceIdType.MESH
EMPTY = 4 * ROWS


def lowest_of(segment):
    return jnp.clip(segment - 1, 0, NCB - W)


def base_of(segment):
    low = lowest_of(jnp.maximum(segment - 1, 0))
    return jnp.minimum(low - low % 2, 8)


def fused_kernel(
    live, cols_ref, map_ref, p_ref, a_ref, shares_out,
    maps, tab, own, near, far, blocks, beside, tiles, wide, left, turned, partial, product, total, gathered,
    chunks, from_cross, from_axial, ready, units,
    tab_s, load, sent0, got0, sent1, got1, sent2, got2, sent3, got3, sent4, got4, sent5, got5, sent6, got6, flush,
):
    seg = lax.axis_index("axial")
    sec = lax.axis_index("cross")
    core = lax.rem(seg, 2)
    layer = seg // 2
    x = sec // 4
    y = lax.rem(sec, 4)
    sibling = seg + 1 - 2 * core
    beyond = seg - 1 + 2 * core
    has_far = (beyond >= 0) & (beyond < 16)
    beyond = jnp.clip(beyond, 0, 15)
    lane_off = lax.rem(sec, 2) * 64

    def remote(src, dst, send, recv, to):
        return pltpu.make_async_remote_copy(
            src_ref=src, dst_ref=dst, send_sem=send, recv_sem=recv, device_id=to, device_id_type=MESH
        )

    barrier = pltpu.get_barrier_semaphore()
    for d in range(1, 16):
        pl.semaphore_signal(barrier, inc=1, device_id=(lax.rem(seg + d, 16), sec), device_id_type=MESH)
        pl.semaphore_signal(barrier, inc=1, device_id=(seg, lax.rem(sec + d, 16)), device_id_type=MESH)

    def piece(ref, c):
        return ref.at[:, pl.ds(PIECES[c][0], PIECES[c][1] - PIECES[c][0]), :]

    own_loads = [pltpu.make_async_copy(piece(p_ref, c), piece(own, c), load.at[c]) for c in range(CHUNKS)]
    for copy in own_loads:
        copy.start()
    map_loads = []
    for part, near_seg in enumerate((seg, sibling, beyond)):
        start = pl.multiple_of((near_seg * 16 + sec - lax.rem(sec, 2)) * ROWS, 128)
        map_loads.append(pltpu.make_async_copy(map_ref.at[:, pl.ds(start, 128)], maps.at[part], load.at[CHUNKS + part]))
        map_loads[part].start()

    def block_load(c):
        return pltpu.make_async_copy(a_ref.at[pl.ds(16 * c, 16)], blocks.at[c % 2], load.at[CHUNKS + 3 + c])

    for c in range(2):
        block_load(c).start()

    def near_copy():
        return remote(own, near, sent0.at[CHUNKS], got0.at[CHUNKS], (sibling, sec))

    def far_copy(c):
        return remote(piece(own, c), piece(far, c), sent0.at[c], got0.at[c], (beyond, sec))

    in_use = live[0, 0]
    for c, (lo, hi) in enumerate(PIECES):
        own_loads[c].wait()

        @pl.loop(0, ROWS, unroll=8)
        def _(row, lo=lo, hi=hi):
            own[row, lo:hi, :] = jnp.where(row < in_use, own[row, lo:hi, :], jnp.zeros((hi - lo, 256), jnp.bfloat16))

        if c == 0:
            pl.semaphore_wait(barrier, 30)

        @pl.when(has_far)
        def _(c=c):
            far_copy(c).start()

    near_copy().start()

    slot = lax.broadcasted_iota(jnp.int32, (8, 128), 0)
    local = lax.broadcasted_iota(jnp.int32, (8, 128), 1) - lane_off
    odd = lax.rem(slot, 2)

    def find(labels, first):
        found = jnp.full((8, 128), EMPTY, jnp.int32)
        for b in range(4):
            even_tile, odd_tile = (0, 2, 1, 3)[b], (2, 0, 3, 1)[b]
            tile = even_tile + odd * (odd_tile - even_tile)
            found = jnp.where(labels[b : b + 1, :] - first == slot, 4 * local + tile, found)
        return found

    base = base_of(seg)
    for part in range(3):
        map_loads[part].wait()
        labels = maps[part]
        tab[part] = find(labels, base)
        if part == 0:
            tab[3] = find(labels, lowest_of(seg))
    named = cols_ref[...]
    named_seg = lax.shift_right_logical(named, 10)
    part = jnp.where(named_seg == seg, 0, jnp.where(named_seg == sibling, 1, 2))
    tab[4, :, 0:64] = part * ROWS + (named & 63)
    tab[4, :, 64:128] = jnp.zeros((8, 64), jnp.int32)
    to_smem = pltpu.make_async_copy(tab, tab_s, load.at[CHUNKS + 7])
    to_smem.start()

    lane_low = lax.broadcasted_iota(jnp.int32, (64, 128), 1) < 64
    tiles[EMPTY] = jnp.zeros((64, 128), jnp.bfloat16)

    def half_tiles(which, row, pair, lo, hi):
        return jnp.where(
            lane_low[lo:hi, :],
            tiles[tab_s[which, 2 * pair, lane_off + row], lo:hi, :],
            tiles[tab_s[which, 2 * pair + 1, lane_off + row], lo:hi, :],
        )

    def store_tiles(source, lo, hi):
        @pl.loop(0, ROWS, unroll=4)
        def _(row):
            value = source[row, lo:hi, :]
            for pair in range(2):
                tile = value[:, 128 * pair : 128 * pair + 128]
                tiles[4 * row + pair, lo:hi, :] = tile
                tiles[4 * row + 2 + pair, lo:hi, :] = jnp.concatenate([tile[:, 64:], tile[:, :64]], axis=1)

    def widen(part, lo, hi):
        @pl.loop(0, ROWS, unroll=4)
        def _(row):
            for pair in range(4):
                wide[part * ROWS + row, lo:hi, 128 * pair : 128 * pair + 128] = half_tiles(part, row, pair, lo, hi)

    store_tiles(own, 0, 64)
    to_smem.wait()
    widen(0, 0, 64)

    @pl.loop(0, 8)
    def _(group):
        for inner in range(8):
            for pair in range(3):
                left[64 * inner : 64 * inner + 64, 128 * pair : 128 * pair + 128] = half_tiles(
                    3, group * 8 + inner, pair, 0, 64
                )
        turned[group] = left[...].T

    for c in range(4):
        block_load(c).wait()

        @pl.loop(0, 16, unroll=2)
        def _(row, c=c):
            at = 0
            for lo, hi in PIECES:
                width = 8 * (hi - lo)
                beside[16 * c + row, :, at : at + width] = jnp.concatenate(
                    [blocks[c % 2, row, k][:, lo:hi] for k in range(8)], axis=1
                )
                at += width

        if c < 2:
            block_load(c + 2).start()

    near_copy().wait_recv()
    store_tiles(near, 0, 64)
    widen(1, 0, 64)

    for c, (lo, hi) in enumerate(PIECES):

        @pl.when(has_far)
        def _(c=c, lo=lo, hi=hi):
            far_copy(c).wait_recv()
            store_tiles(far, lo, hi)
            widen(2, lo, hi)

        @pl.loop(0, ROWS, unroll=8)
        def _(row, c=c, lo=lo, hi=hi):
            rhs = jnp.concatenate([wide[tab_s[4, k, row], lo:hi, :] for k in range(8)], axis=0)
            term = jnp.dot(beside[row, :, 8 * lo : 8 * hi], rhs, preferred_element_type=jnp.float32)
            at = pl.ds(pl.multiple_of(row * 64, 64), 64)
            if c > 0:
                term = partial[at, :] + term
            if c < CHUNKS - 1:
                partial[at, :] = term
            else:
                product[at, :] = term.astype(jnp.bfloat16)

    def cross_send(target):
        return remote(chunks.at[target], from_cross.at[sec], sent1.at[target], got1.at[sec], (seg, target))

    for half in range(2):
        columns = slice(256 * half, 256 * half + 256)
        value = None
        for group in range(8):
            term = jnp.dot(
                turned[group], product[512 * group : 512 * group + 512, columns], preferred_element_type=jnp.float32
            )
            value = term if value is None else value + term
        total[...] = value

        for quarter in range(4):
            for pair in range(2):
                target = quarter * 4 + lax.rem(base // 2 + 2 * half + pair, 4)
                for block in range(W):
                    at = block * 64 + quarter * 16
                    chunks[target, block * 16 : block * 16 + 16, :] = total[
                        at : at + 16, 128 * pair : 128 * pair + 128
                    ].astype(jnp.bfloat16)

                @pl.when(target != sec)
                def _(target=target):
                    cross_send(target).start()

    value = chunks[sec].astype(jnp.float32)
    for d in range(1, 16):
        source = lax.rem(sec + d, 16)
        remote(chunks.at[source], from_cross.at[source], sent1.at[source], got1.at[source], (seg, source)).wait_recv()
        value = value + from_cross[source].astype(jnp.float32)
    units[0:80, :] = value
    units[80:112, :] = jnp.zeros((32, 128), jnp.float32)

    def half_of(segment):
        start = base_of(segment) // 2
        return (start + lax.rem(y - start + 8, 4)) // 4

    my_half = half_of(seg)
    my_low = lowest_of(seg)

    def axial_copy(i):
        block = my_low + i
        owner = (block // 2) * 2 + my_half
        place = lax.rem(block, 2)
        copy = remote(
            units.at[pl.ds(16 * i, 16)], from_axial.at[seg, place], sent2.at[i], got2.at[seg, place], (owner, sec)
        )
        return owner, place, copy

    for i in range(W):
        owner, place, copy = axial_copy(i)

        @pl.when(owner != seg)
        def _(copy=copy):
            copy.start()

        @pl.when(owner == seg)
        def _(i=i, place=place):
            from_axial[seg, place] = units[16 * i : 16 * i + 16, :]

    @pl.loop(0, 16)
    def _(source):
        low = lowest_of(source)
        for place in range(2):
            block = 2 * layer + place

            @pl.when((half_of(source) == core) & (block >= low) & (block < low + W))
            def _(place=place):
                @pl.when(source != seg)
                def _():
                    remote(
                        units.at[pl.ds(0, 16)],
                        from_axial.at[source, place],
                        sent2.at[0],
                        got2.at[source, place],
                        (sibling, sec),
                    ).wait_recv()

                units[80 + 16 * place : 96 + 16 * place, :] += from_axial[source, place]

    mine = pl.ds(pl.multiple_of(layer * 32, 32), 32)
    ready[mine, :] = units[80:112, :].astype(jnp.bfloat16)

    def layer_copy(d):
        return remote(ready.at[mine], ready.at[mine], sent3.at[d], got3.at[d], (lax.rem(seg + 2 * d, 16), sec))

    for d in range(1, 8):
        layer_copy(d).start()
    for d in range(1, 8):
        source = pl.ds(pl.multiple_of(lax.rem(layer - d + 8, 8) * 32, 32), 32)
        remote(ready.at[source], ready.at[source], sent3.at[d], got3.at[d], (sibling, sec)).wait_recv()

    first = jnp.where(core == 0, y // 3, jnp.minimum(3 + y, 4))
    gathered[0, y, x] = ready[pl.ds(pl.multiple_of(first * 16, 16), 96), :]
    gathered[1, x, y] = ready[pl.ds(pl.multiple_of(first * 16 + 96, 16), 96), :]

    def moved(which, d):
        return (seg, lax.rem(x + d, 4) * 4 + y) if which == 0 else (seg, x * 4 + lax.rem(y + d, 4))

    def back(which, d):
        return lax.rem((x if which == 0 else y) - d + 4, 4)

    def one_copy(which, d):
        major, minor = (y, x) if which == 0 else (x, y)
        share = gathered.at[which, major, minor]
        return remote(share, share, sent4.at[which, d], got4.at[which, d], moved(which, d))

    def four_copy(which, d):
        shares = gathered.at[which, y if which == 0 else x]
        return remote(shares, shares, sent5.at[which, d], got5.at[which, d], moved(1 - which, d))

    def pass_copy(half, which, d):
        place = back(1 - which, d)
        shares = gathered.at[which, place]
        return remote(shares, shares_out.at[half, which, place], sent6.at[which, d], got6.at[which, d], (sibling, sec))

    def keep_copy(which, d):
        place = back(1 - which, d)
        return pltpu.make_async_copy(gathered.at[which, place], shares_out.at[core, which, place], flush.at[which, d])

    for d in (2, 1, 3):
        for which in range(2):
            one_copy(which, d).start()
    for which in range(2):
        for d in (1, 3, 2):
            share = gathered.at[which, y if which == 0 else x, back(which, d)]
            remote(share, share, sent4.at[which, d], got4.at[which, d], (sibling, sec)).wait_recv()
        for d in (2, 1, 3):
            four_copy(which, d).start()
    for which in range(2):
        pass_copy(core, which, 0).start()
        keep_copy(which, 0).start()
    for d in (1, 3, 2):
        for which in range(2):
            shares = gathered.at[which, back(1 - which, d)]
            remote(shares, shares, sent5.at[which, d], got5.at[which, d], (sibling, sec)).wait_recv()
            pass_copy(core, which, d).start()
            keep_copy(which, d).start()
    for which in range(2):
        for d in range(4):
            pass_copy(1 - core, which, d).wait_recv()

    near_copy().wait_send()
    for c in range(CHUNKS):

        @pl.when(has_far)
        def _(c=c):
            far_copy(c).wait_send()

    for d in range(1, 16):
        cross_send(lax.rem(sec + d, 16)).wait_send()
    for i in range(W):
        owner, _, copy = axial_copy(i)

        @pl.when(owner != seg)
        def _(copy=copy):
            copy.wait_send()

    for d in range(1, 8):
        layer_copy(d).wait_send()
    for which in range(2):
        for d in range(1, 4):
            one_copy(which, d).wait_send()
            four_copy(which, d).wait_send()
        for d in range(4):
            pass_copy(core, which, d).wait_send()
            keep_copy(which, d).wait()


def fused(live, cols, coarse, prolong, operator):
    dma = pltpu.SemaphoreType.DMA
    vmem = pl.BlockSpec(memory_space=pltpu.VMEM)
    anywhere = pl.BlockSpec(memory_space=pl.ANY)
    bf16, f32, i32 = jnp.bfloat16, jnp.float32, jnp.int32
    return pl.pallas_call(
        fused_kernel,
        out_shape=jax.ShapeDtypeStruct((2, 2, 4, 4, 96, 128), bf16),
        in_specs=[pl.BlockSpec(memory_space=pltpu.SMEM), vmem, anywhere, anywhere, anywhere],
        out_specs=anywhere,
        scratch_shapes=[
            pltpu.VMEM((3, 4, 128), i32),
            pltpu.VMEM((5, 8, 128), i32),
            pltpu.VMEM((ROWS, 64, 256), bf16),
            pltpu.VMEM((ROWS, 64, 256), bf16),
            pltpu.VMEM((ROWS, 64, 256), bf16),
            pltpu.VMEM((2, 16, 8, 64, 64), bf16),
            pltpu.VMEM((ROWS, 64, 512), bf16),
            pltpu.VMEM((4 * ROWS + 1, 64, 128), bf16),
            pltpu.VMEM((3 * ROWS, 64, 512), bf16),
            pltpu.VMEM((512, 384), bf16),
            pltpu.VMEM((8, 384, 512), bf16),
            pltpu.VMEM((ROWS * 64, 512), f32),
            pltpu.VMEM((ROWS * 64, 512), bf16),
            pltpu.VMEM((384, 256), f32),
            pltpu.VMEM((2, 4, 4, 96, 128), bf16),
            pltpu.VMEM((16, 80, 128), bf16),
            pltpu.VMEM((16, 80, 128), bf16),
            pltpu.VMEM((16, 2, 16, 128), f32),
            pltpu.VMEM((256, 128), bf16),
            pltpu.VMEM((112, 128), f32),
            pltpu.SMEM((5, 8, 128), i32),
            dma((CHUNKS + 8,)),
            dma((CHUNKS + 1,)),
            dma((CHUNKS + 1,)),
            dma((16,)),
            dma((16,)),
            dma((W,)),
            dma((16, 2)),
            dma((8,)),
            dma((8,)),
            dma((2, 4)),
            dma((2, 4)),
            dma((2, 4)),
            dma((2, 4)),
            dma((2, 4)),
            dma((2, 4)),
            dma((2, 4)),
        ],
        compiler_params=pltpu.CompilerParams(collective_id=0, has_side_effects=True, vmem_limit_bytes=61 * 2**20),
        name="fused",
    )(live, cols, coarse, prolong, operator)


def place_kernel(first_share, second_share, out_ref):
    half, low_y = pl.program_id(0) // 2, lax.rem(pl.program_id(0), 2) * 2
    out_ref[...] = jnp.zeros_like(out_ref)
    for j in range(2):
        y = low_y + j
        first = jnp.where(half == 0, y // 3, jnp.minimum(3 + y, 4))
        for x in range(4):
            for unit in range(12):
                row = pl.multiple_of((first + unit) * 64 + x * 16, 16)
                rows = slice(unit % 6 * 16, unit % 6 * 16 + 16)
                value = first_share[0, 0, j, x, rows, :] if unit < 6 else second_share[0, 0, x, j, rows, :]
                out_ref[pl.ds(row, 16), 128 * j : 128 * j + 128] = value.astype(jnp.float32)


def place(shares):
    return pl.pallas_call(
        place_kernel,
        grid=(4,),
        out_shape=jax.ShapeDtypeStruct((1024, 1024), jnp.float32),
        in_specs=[
            pl.BlockSpec((1, 1, 2, 4, 96, 128), lambda i: (i // 2, 0, i % 2, 0, 0, 0)),
            pl.BlockSpec((1, 1, 4, 2, 96, 128), lambda i: (i // 2, 1, 0, i % 2, 0, 0)),
        ],
        out_specs=pl.BlockSpec((1024, 256), lambda i: (0, i)),
        compiler_params=pltpu.CompilerParams(vmem_limit_bytes=61 * 2**20),
        name="place",
    )(shares, shares)


def on_device(operator_blocks, prolong_blocks, operator_cols, coarse_map, live_rows):
    shares = fused(live_rows, operator_cols[0, 0].T, coarse_map.T, prolong_blocks[0, 0], operator_blocks[0, 0])
    return place(shares)


def solution(mesh):
    return jax.shard_map(
        on_device,
        mesh=mesh,
        in_specs=(
            P("axial", "cross", None, None, None, None),
            P("axial", "cross", None, None, None),
            P("axial", "cross", None, None),
            P(),
            P("axial", "cross"),
        ),
        out_specs=P(),
        check_vma=False,
    )
```

```python
import jax
import jax.numpy as jnp
from jax import lax
from jax.experimental import pallas as pl
from jax.experimental.pallas import tpu as pltpu
from jax.sharding import PartitionSpec as P

NCB = 16
W = 5
ROWS = 64
PIECES = ((0, 32), (32, 64))
CHUNKS = len(PIECES)
MESH = pl.DeviceIdType.MESH
EMPTY = 4 * ROWS


def lowest_of(segment):
    return jnp.clip(segment - 1, 0, NCB - W)


def base_of(segment):
    low = lowest_of(jnp.maximum(segment - 1, 0))
    return jnp.minimum(low - low % 2, 8)


def fused_kernel(
    live, cols_ref, map_ref, p_ref, a_ref, shares_out,
    maps, tab, own, near, far, blocks, beside, tiles, wide, left, turned, partial, product, total, gathered,
    chunks, from_cross, from_axial, ready, units,
    tab_s, load, sent0, got0, sent1, got1, sent2, got2, sent3, got3, sent4, got4, sent5, got5, sent6, got6, flush,
):
    seg = lax.axis_index("axial")
    sec = lax.axis_index("cross")
    core = lax.rem(seg, 2)
    layer = seg // 2
    x = sec // 4
    y = lax.rem(sec, 4)
    sibling = seg + 1 - 2 * core
    beyond = seg - 1 + 2 * core
    has_far = (beyond >= 0) & (beyond < 16)
    beyond = jnp.clip(beyond, 0, 15)
    lane_off = lax.rem(sec, 2) * 64

    def remote(src, dst, send, recv, to):
        return pltpu.make_async_remote_copy(
            src_ref=src, dst_ref=dst, send_sem=send, recv_sem=recv, device_id=to, device_id_type=MESH
        )

    barrier = pltpu.get_barrier_semaphore()
    for d in range(1, 16):
        pl.semaphore_signal(barrier, inc=1, device_id=(lax.rem(seg + d, 16), sec), device_id_type=MESH)
        pl.semaphore_signal(barrier, inc=1, device_id=(seg, lax.rem(sec + d, 16)), device_id_type=MESH)

    def piece(ref, c):
        return ref.at[:, pl.ds(PIECES[c][0], PIECES[c][1] - PIECES[c][0]), :]

    own_loads = [pltpu.make_async_copy(piece(p_ref, c), piece(own, c), load.at[c]) for c in range(CHUNKS)]
    for copy in own_loads:
        copy.start()
    map_loads = []
    for part, near_seg in enumerate((seg, sibling, beyond)):
        start = pl.multiple_of((near_seg * 16 + sec - lax.rem(sec, 2)) * ROWS, 128)
        map_loads.append(pltpu.make_async_copy(map_ref.at[:, pl.ds(start, 128)], maps.at[part], load.at[CHUNKS + part]))
        map_loads[part].start()

    def block_load(c):
        return pltpu.make_async_copy(a_ref.at[pl.ds(16 * c, 16)], blocks.at[c % 2], load.at[CHUNKS + 3 + c])

    for c in range(2):
        block_load(c).start()

    def near_copy():
        return remote(own, near, sent0.at[CHUNKS], got0.at[CHUNKS], (sibling, sec))

    def far_copy(c):
        return remote(piece(own, c), piece(far, c), sent0.at[c], got0.at[c], (beyond, sec))

    in_use = live[0, 0]
    for c, (lo, hi) in enumerate(PIECES):
        own_loads[c].wait()

        @pl.loop(0, ROWS, unroll=8)
        def _(row, lo=lo, hi=hi):
            own[row, lo:hi, :] = jnp.where(row < in_use, own[row, lo:hi, :], jnp.zeros((hi - lo, 256), jnp.bfloat16))

        if c == 0:
            pl.semaphore_wait(barrier, 30)

        @pl.when(has_far)
        def _(c=c):
            far_copy(c).start()

    near_copy().start()

    slot = lax.broadcasted_iota(jnp.int32, (8, 128), 0)
    local = lax.broadcasted_iota(jnp.int32, (8, 128), 1) - lane_off
    odd = lax.rem(slot, 2)

    def find(labels, first):
        found = jnp.full((8, 128), EMPTY, jnp.int32)
        for b in range(4):
            even_tile, odd_tile = (0, 2, 1, 3)[b], (2, 0, 3, 1)[b]
            tile = even_tile + odd * (odd_tile - even_tile)
            found = jnp.where(labels[b : b + 1, :] - first == slot, 4 * local + tile, found)
        return found

    base = base_of(seg)
    for part in range(3):
        map_loads[part].wait()
        labels = maps[part]
        tab[part] = find(labels, base)
        if part == 0:
            tab[3] = find(labels, lowest_of(seg))
    named = cols_ref[...]
    named_seg = lax.shift_right_logical(named, 10)
    part = jnp.where(named_seg == seg, 0, jnp.where(named_seg == sibling, 1, 2))
    tab[4, :, 0:64] = part * ROWS + (named & 63)
    tab[4, :, 64:128] = jnp.zeros((8, 64), jnp.int32)
    to_smem = pltpu.make_async_copy(tab, tab_s, load.at[CHUNKS + 7])
    to_smem.start()

    lane_low = lax.broadcasted_iota(jnp.int32, (64, 128), 1) < 64
    tiles[EMPTY] = jnp.zeros((64, 128), jnp.bfloat16)

    def half_tiles(which, row, pair, lo, hi):
        return jnp.where(
            lane_low[lo:hi, :],
            tiles[tab_s[which, 2 * pair, lane_off + row], lo:hi, :],
            tiles[tab_s[which, 2 * pair + 1, lane_off + row], lo:hi, :],
        )

    def store_tiles(source, lo, hi):
        @pl.loop(0, ROWS, unroll=8)
        def _(row):
            value = source[row, lo:hi, :]
            for pair in range(2):
                tile = value[:, 128 * pair : 128 * pair + 128]
                tiles[4 * row + pair, lo:hi, :] = tile
                tiles[4 * row + 2 + pair, lo:hi, :] = jnp.concatenate([tile[:, 64:], tile[:, :64]], axis=1)

    def widen(part, lo, hi):
        @pl.loop(0, ROWS, unroll=8)
        def _(row):
            for pair in range(4):
                wide[part * ROWS + row, lo:hi, 128 * pair : 128 * pair + 128] = half_tiles(part, row, pair, lo, hi)

    store_tiles(own, 0, 64)
    to_smem.wait()
    widen(0, 0, 64)

    @pl.loop(0, 8)
    def _(group):
        for inner in range(8):
            for pair in range(3):
                left[64 * inner : 64 * inner + 64, 128 * pair : 128 * pair + 128] = half_tiles(
                    3, group * 8 + inner, pair, 0, 64
                )
        turned[group] = left[...].T

    for c in range(4):
        block_load(c).wait()

        @pl.loop(0, 16, unroll=2)
        def _(row, c=c):
            at = 0
            for lo, hi in PIECES:
                width = 8 * (hi - lo)
                beside[16 * c + row, :, at : at + width] = jnp.concatenate(
                    [blocks[c % 2, row, k][:, lo:hi] for k in range(8)], axis=1
                )
                at += width

        if c < 2:
            block_load(c + 2).start()

    near_copy().wait_recv()
    store_tiles(near, 0, 64)
    widen(1, 0, 64)

    for c, (lo, hi) in enumerate(PIECES):

        @pl.when(has_far)
        def _(c=c, lo=lo, hi=hi):
            far_copy(c).wait_recv()
            store_tiles(far, lo, hi)
            widen(2, lo, hi)

        @pl.loop(0, ROWS, unroll=16)
        def _(row, c=c, lo=lo, hi=hi):
            rhs = jnp.concatenate([wide[tab_s[4, k, row], lo:hi, :] for k in range(8)], axis=0)
            term = jnp.dot(beside[row, :, 8 * lo : 8 * hi], rhs, preferred_element_type=jnp.float32)
            at = pl.ds(pl.multiple_of(row * 64, 64), 64)
            if c > 0:
                term = partial[at, :] + term
            if c < CHUNKS - 1:
                partial[at, :] = term
            else:
                product[at, :] = term.astype(jnp.bfloat16)

    def cross_send(target):
        return remote(chunks.at[target], from_cross.at[sec], sent1.at[target], got1.at[sec], (seg, target))

    for half in range(2):
        columns = slice(256 * half, 256 * half + 256)
        value = None
        for group in range(8):
            term = jnp.dot(
                turned[group], product[512 * group : 512 * group + 512, columns], preferred_element_type=jnp.float32
            )
            value = term if value is None else value + term
        total[...] = value

        for quarter in range(4):
            for pair in range(2):
                target = quarter * 4 + lax.rem(base // 2 + 2 * half + pair, 4)
                for block in range(W):
                    at = block * 64 + quarter * 16
                    chunks[target, block * 16 : block * 16 + 16, :] = total[
                        at : at + 16, 128 * pair : 128 * pair + 128
                    ].astype(jnp.bfloat16)

                @pl.when(target != sec)
                def _(target=target):
                    cross_send(target).start()

    value = chunks[sec].astype(jnp.float32)
    for d in range(1, 16):
        source = lax.rem(sec + d, 16)
        remote(chunks.at[source], from_cross.at[source], sent1.at[source], got1.at[source], (seg, source)).wait_recv()
        value = value + from_cross[source].astype(jnp.float32)
    units[0:80, :] = value
    units[80:112, :] = jnp.zeros((32, 128), jnp.float32)

    def half_of(segment):
        start = base_of(segment) // 2
        return (start + lax.rem(y - start + 8, 4)) // 4

    my_half = half_of(seg)
    my_low = lowest_of(seg)

    def axial_copy(i):
        block = my_low + i
        owner = (block // 2) * 2 + my_half
        place = lax.rem(block, 2)
        copy = remote(
            units.at[pl.ds(16 * i, 16)], from_axial.at[seg, place], sent2.at[i], got2.at[seg, place], (owner, sec)
        )
        return owner, place, copy

    for i in range(W):
        owner, place, copy = axial_copy(i)

        @pl.when(owner != seg)
        def _(copy=copy):
            copy.start()

        @pl.when(owner == seg)
        def _(i=i, place=place):
            from_axial[seg, place] = units[16 * i : 16 * i + 16, :]

    @pl.loop(0, 16)
    def _(source):
        low = lowest_of(source)
        for place in range(2):
            block = 2 * layer + place

            @pl.when((half_of(source) == core) & (block >= low) & (block < low + W))
            def _(place=place):
                @pl.when(source != seg)
                def _():
                    remote(
                        units.at[pl.ds(0, 16)],
                        from_axial.at[source, place],
                        sent2.at[0],
                        got2.at[source, place],
                        (sibling, sec),
                    ).wait_recv()

                units[80 + 16 * place : 96 + 16 * place, :] += from_axial[source, place]

    mine = pl.ds(pl.multiple_of(layer * 32, 32), 32)
    ready[mine, :] = units[80:112, :].astype(jnp.bfloat16)

    def layer_copy(d):
        return remote(ready.at[mine], ready.at[mine], sent3.at[d], got3.at[d], (lax.rem(seg + 2 * d, 16), sec))

    for d in range(1, 8):
        layer_copy(d).start()
    for d in range(1, 8):
        source = pl.ds(pl.multiple_of(lax.rem(layer - d + 8, 8) * 32, 32), 32)
        remote(ready.at[source], ready.at[source], sent3.at[d], got3.at[d], (sibling, sec)).wait_recv()

    first = jnp.where(core == 0, y // 3, jnp.minimum(3 + y, 4))
    gathered[0, y, x] = ready[pl.ds(pl.multiple_of(first * 16, 16), 96), :]
    gathered[1, x, y] = ready[pl.ds(pl.multiple_of(first * 16 + 96, 16), 96), :]

    def moved(which, d):
        return (seg, lax.rem(x + d, 4) * 4 + y) if which == 0 else (seg, x * 4 + lax.rem(y + d, 4))

    def back(which, d):
        return lax.rem((x if which == 0 else y) - d + 4, 4)

    def one_copy(which, d):
        major, minor = (y, x) if which == 0 else (x, y)
        share = gathered.at[which, major, minor]
        return remote(share, share, sent4.at[which, d], got4.at[which, d], moved(which, d))

    def next_copy(which, d, j):
        share = gathered.at[which, y if which == 0 else x, back(which, j)]
        return remote(share, share, sent5.at[which, d, j], got5.at[which, d, j], moved(1 - which, d))

    def pass_copy(half, which, d):
        place = back(1 - which, d)
        shares = gathered.at[which, place]
        return remote(shares, shares_out.at[half, which, place], sent6.at[which, d], got6.at[which, d], (sibling, sec))

    def keep_copy(which, d):
        place = back(1 - which, d)
        return pltpu.make_async_copy(gathered.at[which, place], shares_out.at[core, which, place], flush.at[which, d])

    for d in (2, 1, 3):
        for which in range(2):
            one_copy(which, d).start()
    for d in (2, 1, 3):
        for which in range(2):
            next_copy(which, d, 0).start()
    for j in (1, 3, 2):
        for which in range(2):
            share = gathered.at[which, y if which == 0 else x, back(which, j)]
            remote(share, share, sent4.at[which, j], got4.at[which, j], (sibling, sec)).wait_recv()
            for d in (2, 1, 3):
                next_copy(which, d, j).start()
    for which in range(2):
        pass_copy(core, which, 0).start()
        keep_copy(which, 0).start()
    for d in (1, 3, 2):
        for which in range(2):
            for j in (0, 1, 3, 2):
                share = gathered.at[which, back(1 - which, d), back(which, j)]
                remote(share, share, sent5.at[which, d, j], got5.at[which, d, j], (sibling, sec)).wait_recv()
            pass_copy(core, which, d).start()
            keep_copy(which, d).start()
    for which in range(2):
        for d in range(4):
            pass_copy(1 - core, which, d).wait_recv()

    near_copy().wait_send()
    for c in range(CHUNKS):

        @pl.when(has_far)
        def _(c=c):
            far_copy(c).wait_send()

    for d in range(1, 16):
        cross_send(lax.rem(sec + d, 16)).wait_send()
    for i in range(W):
        owner, _, copy = axial_copy(i)

        @pl.when(owner != seg)
        def _(copy=copy):
            copy.wait_send()

    for d in range(1, 8):
        layer_copy(d).wait_send()
    for which in range(2):
        for d in range(1, 4):
            one_copy(which, d).wait_send()
            for j in range(4):
                next_copy(which, d, j).wait_send()
        for d in range(4):
            pass_copy(core, which, d).wait_send()
            keep_copy(which, d).wait()


def fused(live, cols, coarse, prolong, operator):
    dma = pltpu.SemaphoreType.DMA
    vmem = pl.BlockSpec(memory_space=pltpu.VMEM)
    anywhere = pl.BlockSpec(memory_space=pl.ANY)
    bf16, f32, i32 = jnp.bfloat16, jnp.float32, jnp.int32
    return pl.pallas_call(
        fused_kernel,
        out_shape=jax.ShapeDtypeStruct((2, 2, 4, 4, 96, 128), bf16),
        in_specs=[pl.BlockSpec(memory_space=pltpu.SMEM), vmem, anywhere, anywhere, anywhere],
        out_specs=anywhere,
        scratch_shapes=[
            pltpu.VMEM((3, 4, 128), i32),
            pltpu.VMEM((5, 8, 128), i32),
            pltpu.VMEM((ROWS, 64, 256), bf16),
            pltpu.VMEM((ROWS, 64, 256), bf16),
            pltpu.VMEM((ROWS, 64, 256), bf16),
            pltpu.VMEM((2, 16, 8, 64, 64), bf16),
            pltpu.VMEM((ROWS, 64, 512), bf16),
            pltpu.VMEM((4 * ROWS + 1, 64, 128), bf16),
            pltpu.VMEM((3 * ROWS, 64, 512), bf16),
            pltpu.VMEM((512, 384), bf16),
            pltpu.VMEM((8, 384, 512), bf16),
            pltpu.VMEM((ROWS * 64, 512), f32),
            pltpu.VMEM((ROWS * 64, 512), bf16),
            pltpu.VMEM((384, 256), f32),
            pltpu.VMEM((2, 4, 4, 96, 128), bf16),
            pltpu.VMEM((16, 80, 128), bf16),
            pltpu.VMEM((16, 80, 128), bf16),
            pltpu.VMEM((16, 2, 16, 128), f32),
            pltpu.VMEM((256, 128), bf16),
            pltpu.VMEM((112, 128), f32),
            pltpu.SMEM((5, 8, 128), i32),
            dma((CHUNKS + 8,)),
            dma((CHUNKS + 1,)),
            dma((CHUNKS + 1,)),
            dma((16,)),
            dma((16,)),
            dma((W,)),
            dma((16, 2)),
            dma((8,)),
            dma((8,)),
            dma((2, 4)),
            dma((2, 4)),
            dma((2, 4, 4)),
            dma((2, 4, 4)),
            dma((2, 4)),
            dma((2, 4)),
            dma((2, 4)),
        ],
        compiler_params=pltpu.CompilerParams(collective_id=0, has_side_effects=True, vmem_limit_bytes=61 * 2**20),
        name="fused",
    )(live, cols, coarse, prolong, operator)


def place_kernel(shares, out_ref, held, dense, got, gone):
    loads = [pltpu.make_async_copy(shares.at[i // 2, i % 2], held.at[i // 2, i % 2], got.at[i]) for i in range(4)]
    for load in loads:
        load.start()
    windows = {(half, y): y // 3 if half == 0 else min(3 + y, 4) for half in range(2) for y in range(4)}
    for (half, y), first in windows.items():
        column = (y + 4 * half) * 128
        for start, end in ((0, first * 64), ((first + 12) * 64, 1024)):
            if end > start:
                dense[start:end, column : column + 128] = jnp.zeros((end - start, 128), jnp.float32)
    for load in loads:
        load.wait()

    def store(part):
        rows = pl.ds(part * 128, 128)
        return pltpu.make_async_copy(dense.at[rows], out_ref.at[rows], gone.at[part])

    for part in range(8):
        for block in (2 * part, 2 * part + 1):
            for (half, y), first in windows.items():
                unit, column = block - first, (y + 4 * half) * 128
                if not 0 <= unit < 12:
                    continue
                for x in range(4):
                    row = block * 64 + x * 16
                    at = (half, 0, y, x) if unit < 6 else (half, 1, x, y)
                    dense[row : row + 16, column : column + 128] = held[
                        (*at, slice(unit % 6 * 16, unit % 6 * 16 + 16), slice(None))
                    ].astype(jnp.float32)
        store(part).start()
    for part in range(8):
        store(part).wait()


def place(shares):
    anywhere = pl.BlockSpec(memory_space=pl.ANY)
    return pl.pallas_call(
        place_kernel,
        out_shape=jax.ShapeDtypeStruct((1024, 1024), jnp.float32),
        in_specs=[anywhere],
        out_specs=anywhere,
        scratch_shapes=[
            pltpu.VMEM((2, 2, 4, 4, 96, 128), jnp.bfloat16),
            pltpu.VMEM((1024, 1024), jnp.float32),
            pltpu.SemaphoreType.DMA((4,)),
            pltpu.SemaphoreType.DMA((8,)),
        ],
        compiler_params=pltpu.CompilerParams(vmem_limit_bytes=61 * 2**20),
        name="place",
    )(shares)


def on_device(operator_blocks, prolong_blocks, operator_cols, coarse_map, live_rows):
    shares = fused(live_rows, operator_cols[0, 0].T, coarse_map.T, prolong_blocks[0, 0], operator_blocks[0, 0])
    return place(shares)


def solution(mesh):
    return jax.shard_map(
        on_device,
        mesh=mesh,
        in_specs=(
            P("axial", "cross", None, None, None, None),
            P("axial", "cross", None, None, None),
            P("axial", "cross", None, None),
            P(),
            P("axial", "cross"),
        ),
        out_specs=P(),
        check_vma=False,
    )
```

```python
import jax
import jax.numpy as jnp
from jax import lax
from jax.experimental import pallas as pl
from jax.experimental.pallas import tpu as pltpu
from jax.sharding import PartitionSpec as P

NCB = 16
W = 5
ROWS = 64
PIECES = ((0, 32), (32, 48), (48, 64))
CHUNKS = len(PIECES)
MESH = pl.DeviceIdType.MESH
EMPTY = 4 * ROWS


def lowest_of(segment):
    return jnp.clip(segment - 1, 0, NCB - W)


def base_of(segment):
    low = lowest_of(jnp.maximum(segment - 1, 0))
    return jnp.minimum(low - low % 2, 8)


def fused_kernel(
    live, cols_ref, map_ref, p_ref, a_ref, shares_out,
    maps, tab, own, near, far, blocks, beside, tiles, wide, left, turned, partial, partial2, product, total, gathered,
    chunks, from_cross, from_axial, ready, units,
    tab_s, load, sent0, got0, sent1, got1, sent2, got2, sent3, got3, sent4, got4, sent5, got5, sent6, got6, flush,
):
    seg = lax.axis_index("axial")
    sec = lax.axis_index("cross")
    core = lax.rem(seg, 2)
    layer = seg // 2
    x = sec // 4
    y = lax.rem(sec, 4)
    sibling = seg + 1 - 2 * core
    beyond = seg - 1 + 2 * core
    has_far = (beyond >= 0) & (beyond < 16)
    beyond = jnp.clip(beyond, 0, 15)
    lane_off = lax.rem(sec, 2) * 64

    def remote(src, dst, send, recv, to):
        return pltpu.make_async_remote_copy(
            src_ref=src, dst_ref=dst, send_sem=send, recv_sem=recv, device_id=to, device_id_type=MESH
        )

    barrier = pltpu.get_barrier_semaphore()
    for d in range(1, 16):
        pl.semaphore_signal(barrier, inc=1, device_id=(lax.rem(seg + d, 16), sec), device_id_type=MESH)
        pl.semaphore_signal(barrier, inc=1, device_id=(seg, lax.rem(sec + d, 16)), device_id_type=MESH)

    def piece(ref, c):
        return ref.at[:, pl.ds(PIECES[c][0], PIECES[c][1] - PIECES[c][0]), :]

    own_loads = [pltpu.make_async_copy(piece(p_ref, c), piece(own, c), load.at[c]) for c in range(CHUNKS)]
    for copy in own_loads:
        copy.start()
    map_loads = []
    for part, near_seg in enumerate((seg, sibling, beyond)):
        start = pl.multiple_of((near_seg * 16 + sec - lax.rem(sec, 2)) * ROWS, 128)
        map_loads.append(pltpu.make_async_copy(map_ref.at[:, pl.ds(start, 128)], maps.at[part], load.at[CHUNKS + part]))
        map_loads[part].start()

    def block_load(c):
        return pltpu.make_async_copy(a_ref.at[pl.ds(16 * c, 16)], blocks.at[c % 2], load.at[CHUNKS + 3 + c])

    for c in range(2):
        block_load(c).start()

    def near_copy():
        return remote(own, near, sent0.at[CHUNKS], got0.at[CHUNKS], (sibling, sec))

    def far_copy(c):
        return remote(piece(own, c), piece(far, c), sent0.at[c], got0.at[c], (beyond, sec))

    in_use = live[0, 0]
    for c, (lo, hi) in enumerate(PIECES):
        own_loads[c].wait()

        @pl.loop(0, ROWS, unroll=8)
        def _(row, lo=lo, hi=hi):
            own[row, lo:hi, :] = jnp.where(row < in_use, own[row, lo:hi, :], jnp.zeros((hi - lo, 256), jnp.bfloat16))

        if c == 0:
            pl.semaphore_wait(barrier, 30)

        @pl.when(has_far)
        def _(c=c):
            far_copy(c).start()

    near_copy().start()

    slot = lax.broadcasted_iota(jnp.int32, (8, 128), 0)
    local = lax.broadcasted_iota(jnp.int32, (8, 128), 1) - lane_off
    odd = lax.rem(slot, 2)

    def find(labels, first):
        found = jnp.full((8, 128), EMPTY, jnp.int32)
        for b in range(4):
            even_tile, odd_tile = (0, 2, 1, 3)[b], (2, 0, 3, 1)[b]
            tile = even_tile + odd * (odd_tile - even_tile)
            found = jnp.where(labels[b : b + 1, :] - first == slot, 4 * local + tile, found)
        return found

    base = base_of(seg)
    for part in range(3):
        map_loads[part].wait()
        labels = maps[part]
        tab[part] = find(labels, base)
        if part == 0:
            tab[3] = find(labels, lowest_of(seg))
    named = cols_ref[...]
    named_seg = lax.shift_right_logical(named, 10)
    part = jnp.where(named_seg == seg, 0, jnp.where(named_seg == sibling, 1, 2))
    tab[4, :, 0:64] = part * ROWS + (named & 63)
    tab[4, :, 64:128] = jnp.zeros((8, 64), jnp.int32)
    to_smem = pltpu.make_async_copy(tab, tab_s, load.at[CHUNKS + 7])
    to_smem.start()

    lane_low = lax.broadcasted_iota(jnp.int32, (64, 128), 1) < 64
    tiles[EMPTY] = jnp.zeros((64, 128), jnp.bfloat16)

    def half_tiles(which, row, pair, lo, hi):
        return jnp.where(
            lane_low[lo:hi, :],
            tiles[tab_s[which, 2 * pair, lane_off + row], lo:hi, :],
            tiles[tab_s[which, 2 * pair + 1, lane_off + row], lo:hi, :],
        )

    def store_tiles(source, lo, hi):
        @pl.loop(0, ROWS, unroll=8)
        def _(row):
            value = source[row, lo:hi, :]
            for pair in range(2):
                tile = value[:, 128 * pair : 128 * pair + 128]
                tiles[4 * row + pair, lo:hi, :] = tile
                tiles[4 * row + 2 + pair, lo:hi, :] = jnp.concatenate([tile[:, 64:], tile[:, :64]], axis=1)

    def widen(part, lo, hi):
        @pl.loop(0, ROWS, unroll=8)
        def _(row):
            for pair in range(4):
                wide[part * ROWS + row, lo:hi, 128 * pair : 128 * pair + 128] = half_tiles(part, row, pair, lo, hi)

    store_tiles(own, 0, 64)
    to_smem.wait()
    widen(0, 0, 64)

    @pl.loop(0, 8)
    def _(group):
        for inner in range(8):
            for pair in range(3):
                left[64 * inner : 64 * inner + 64, 128 * pair : 128 * pair + 128] = half_tiles(
                    3, group * 8 + inner, pair, 0, 64
                )
        turned[group] = left[...].T

    for c in range(4):
        block_load(c).wait()

        @pl.loop(0, 16, unroll=2)
        def _(row, c=c):
            at = 0
            for lo, hi in PIECES:
                width = 8 * (hi - lo)
                beside[16 * c + row, :, at : at + width] = jnp.concatenate(
                    [blocks[c % 2, row, k][:, lo:hi] for k in range(8)], axis=1
                )
                at += width

        if c < 2:
            block_load(c + 2).start()

    near_copy().wait_recv()
    store_tiles(near, 0, 64)
    widen(1, 0, 64)

    sums = (partial, partial2)

    for c, (lo, hi) in enumerate(PIECES):

        @pl.when(has_far)
        def _(c=c, lo=lo, hi=hi):
            far_copy(c).wait_recv()
            store_tiles(far, lo, hi)
            widen(2, lo, hi)

        @pl.loop(0, ROWS, unroll=16)
        def _(row, c=c, lo=lo, hi=hi):
            rhs = jnp.concatenate([wide[tab_s[4, k, row], lo:hi, :] for k in range(8)], axis=0)
            term = jnp.dot(beside[row, :, 8 * lo : 8 * hi], rhs, preferred_element_type=jnp.float32)
            at = pl.ds(pl.multiple_of(row * 64, 64), 64)
            if c > 0:
                term = sums[c - 1][at, :] + term
            if c < CHUNKS - 1:
                sums[c][at, :] = term
            else:
                product[at, :] = term.astype(jnp.bfloat16)

    def cross_send(target):
        return remote(chunks.at[target], from_cross.at[sec], sent1.at[target], got1.at[sec], (seg, target))

    for half in range(2):
        columns = slice(256 * half, 256 * half + 256)
        value = None
        for group in range(8):
            term = jnp.dot(
                turned[group], product[512 * group : 512 * group + 512, columns], preferred_element_type=jnp.float32
            )
            value = term if value is None else value + term
        total[...] = value

        for quarter in range(4):
            for pair in range(2):
                target = quarter * 4 + lax.rem(base // 2 + 2 * half + pair, 4)
                for block in range(W):
                    at = block * 64 + quarter * 16
                    chunks[target, block * 16 : block * 16 + 16, :] = total[
                        at : at + 16, 128 * pair : 128 * pair + 128
                    ].astype(jnp.bfloat16)

                @pl.when(target != sec)
                def _(target=target):
                    cross_send(target).start()

    value = chunks[sec].astype(jnp.float32)
    for d in range(1, 16):
        source = lax.rem(sec + d, 16)
        remote(chunks.at[source], from_cross.at[source], sent1.at[source], got1.at[source], (seg, source)).wait_recv()
        value = value + from_cross[source].astype(jnp.float32)
    units[0:80, :] = value
    units[80:112, :] = jnp.zeros((32, 128), jnp.float32)

    def half_of(segment):
        start = base_of(segment) // 2
        return (start + lax.rem(y - start + 8, 4)) // 4

    my_half = half_of(seg)
    my_low = lowest_of(seg)

    def axial_copy(i):
        block = my_low + i
        owner = (block // 2) * 2 + my_half
        place = lax.rem(block, 2)
        copy = remote(
            units.at[pl.ds(16 * i, 16)], from_axial.at[seg, place], sent2.at[i], got2.at[seg, place], (owner, sec)
        )
        return owner, place, copy

    for i in range(W):
        owner, place, copy = axial_copy(i)

        @pl.when(owner != seg)
        def _(copy=copy):
            copy.start()

        @pl.when(owner == seg)
        def _(i=i, place=place):
            from_axial[seg, place] = units[16 * i : 16 * i + 16, :]

    first_source = jnp.where(2 * layer <= 4, 0, 2 * layer - 3)
    end_source = jnp.where(2 * layer + 1 >= NCB - W, 16, 2 * layer + 3)

    @pl.loop(first_source, end_source)
    def _(source):
        low = lowest_of(source)
        for place in range(2):
            block = 2 * layer + place

            @pl.when((half_of(source) == core) & (block >= low) & (block < low + W))
            def _(place=place):
                @pl.when(source != seg)
                def _():
                    remote(
                        units.at[pl.ds(0, 16)],
                        from_axial.at[source, place],
                        sent2.at[0],
                        got2.at[source, place],
                        (sibling, sec),
                    ).wait_recv()

                units[80 + 16 * place : 96 + 16 * place, :] += from_axial[source, place]

    mine = pl.ds(pl.multiple_of(layer * 32, 32), 32)
    ready[mine, :] = units[80:112, :].astype(jnp.bfloat16)

    def layer_copy(d):
        return remote(ready.at[mine], ready.at[mine], sent3.at[d], got3.at[d], (lax.rem(seg + 2 * d, 16), sec))

    for d in range(1, 8):
        layer_copy(d).start()
    for d in range(1, 8):
        source = pl.ds(pl.multiple_of(lax.rem(layer - d + 8, 8) * 32, 32), 32)
        remote(ready.at[source], ready.at[source], sent3.at[d], got3.at[d], (sibling, sec)).wait_recv()

    first = jnp.where(core == 0, y // 3, jnp.minimum(3 + y, 4))
    gathered[0, y, x] = ready[pl.ds(pl.multiple_of(first * 16, 16), 96), :]
    gathered[1, x, y] = ready[pl.ds(pl.multiple_of(first * 16 + 96, 16), 96), :]

    def moved(which, d):
        return (seg, lax.rem(x + d, 4) * 4 + y) if which == 0 else (seg, x * 4 + lax.rem(y + d, 4))

    def back(which, d):
        return lax.rem((x if which == 0 else y) - d + 4, 4)

    def one_copy(which, d):
        major, minor = (y, x) if which == 0 else (x, y)
        share = gathered.at[which, major, minor]
        return remote(share, share, sent4.at[which, d], got4.at[which, d], moved(which, d))

    def next_copy(which, d, j):
        share = gathered.at[which, y if which == 0 else x, back(which, j)]
        return remote(share, share, sent5.at[which, d, j], got5.at[which, d, j], moved(1 - which, d))

    def pass_copy(half, which, d):
        place = back(1 - which, d)
        shares = gathered.at[which, place]
        return remote(shares, shares_out.at[half, which, place], sent6.at[which, d], got6.at[which, d], (sibling, sec))

    def keep_copy(which, d):
        place = back(1 - which, d)
        return pltpu.make_async_copy(gathered.at[which, place], shares_out.at[core, which, place], flush.at[which, d])

    for d in (2, 1, 3):
        for which in range(2):
            one_copy(which, d).start()
    for d in (2, 1, 3):
        for which in range(2):
            next_copy(which, d, 0).start()
    for j in (1, 3, 2):
        for which in range(2):
            share = gathered.at[which, y if which == 0 else x, back(which, j)]
            remote(share, share, sent4.at[which, j], got4.at[which, j], (sibling, sec)).wait_recv()
            for d in (2, 1, 3):
                next_copy(which, d, j).start()
    for which in range(2):
        pass_copy(core, which, 0).start()
        keep_copy(which, 0).start()
    for d in (1, 3, 2):
        for which in range(2):
            for j in (0, 1, 3, 2):
                share = gathered.at[which, back(1 - which, d), back(which, j)]
                remote(share, share, sent5.at[which, d, j], got5.at[which, d, j], (sibling, sec)).wait_recv()
            pass_copy(core, which, d).start()
            keep_copy(which, d).start()
    for which in range(2):
        for d in range(4):
            pass_copy(1 - core, which, d).wait_recv()

    near_copy().wait_send()
    for c in range(CHUNKS):

        @pl.when(has_far)
        def _(c=c):
            far_copy(c).wait_send()

    for d in range(1, 16):
        cross_send(lax.rem(sec + d, 16)).wait_send()
    for i in range(W):
        owner, _, copy = axial_copy(i)

        @pl.when(owner != seg)
        def _(copy=copy):
            copy.wait_send()

    for d in range(1, 8):
        layer_copy(d).wait_send()
    for which in range(2):
        for d in range(1, 4):
            one_copy(which, d).wait_send()
            for j in range(4):
                next_copy(which, d, j).wait_send()
        for d in range(4):
            pass_copy(core, which, d).wait_send()
            keep_copy(which, d).wait()


def fused(live, cols, coarse, prolong, operator):
    dma = pltpu.SemaphoreType.DMA
    vmem = pl.BlockSpec(memory_space=pltpu.VMEM)
    anywhere = pl.BlockSpec(memory_space=pl.ANY)
    bf16, f32, i32 = jnp.bfloat16, jnp.float32, jnp.int32
    return pl.pallas_call(
        fused_kernel,
        out_shape=jax.ShapeDtypeStruct((2, 2, 4, 4, 96, 128), bf16),
        in_specs=[pl.BlockSpec(memory_space=pltpu.SMEM), vmem, anywhere, anywhere, anywhere],
        out_specs=anywhere,
        scratch_shapes=[
            pltpu.VMEM((3, 4, 128), i32),
            pltpu.VMEM((5, 8, 128), i32),
            pltpu.VMEM((ROWS, 64, 256), bf16),
            pltpu.VMEM((ROWS, 64, 256), bf16),
            pltpu.VMEM((ROWS, 64, 256), bf16),
            pltpu.VMEM((2, 16, 8, 64, 64), bf16),
            pltpu.VMEM((ROWS, 64, 512), bf16),
            pltpu.VMEM((4 * ROWS + 1, 64, 128), bf16),
            pltpu.VMEM((3 * ROWS, 64, 512), bf16),
            pltpu.VMEM((512, 384), bf16),
            pltpu.VMEM((8, 384, 512), bf16),
            pltpu.VMEM((ROWS * 64, 512), f32),
            pltpu.VMEM((ROWS * 64, 512), f32),
            pltpu.VMEM((ROWS * 64, 512), bf16),
            pltpu.VMEM((384, 256), f32),
            pltpu.VMEM((2, 4, 4, 96, 128), bf16),
            pltpu.VMEM((16, 80, 128), bf16),
            pltpu.VMEM((16, 80, 128), bf16),
            pltpu.VMEM((16, 2, 16, 128), f32),
            pltpu.VMEM((256, 128), bf16),
            pltpu.VMEM((112, 128), f32),
            pltpu.SMEM((5, 8, 128), i32),
            dma((CHUNKS + 8,)),
            dma((CHUNKS + 1,)),
            dma((CHUNKS + 1,)),
            dma((16,)),
            dma((16,)),
            dma((W,)),
            dma((16, 2)),
            dma((8,)),
            dma((8,)),
            dma((2, 4)),
            dma((2, 4)),
            dma((2, 4, 4)),
            dma((2, 4, 4)),
            dma((2, 4)),
            dma((2, 4)),
            dma((2, 4)),
        ],
        compiler_params=pltpu.CompilerParams(collective_id=0, has_side_effects=True, vmem_limit_bytes=61 * 2**20),
        name="fused",
    )(live, cols, coarse, prolong, operator)


def place_kernel(shares, out_ref, held, dense, got, gone):
    loads = [pltpu.make_async_copy(shares.at[i // 2, i % 2], held.at[i // 2, i % 2], got.at[i]) for i in range(4)]
    for load in loads:
        load.start()
    windows = {(half, y): y // 3 if half == 0 else min(3 + y, 4) for half in range(2) for y in range(4)}
    for (half, y), first in windows.items():
        column = (y + 4 * half) * 128
        for start, end in ((0, first * 64), ((first + 12) * 64, 1024)):
            if end > start:
                dense[start:end, column : column + 128] = jnp.zeros((end - start, 128), jnp.float32)

    def store(half, part):
        area = (pl.ds(part * 256, 256), pl.ds(half * 512, 512))
        return pltpu.make_async_copy(dense.at[area], out_ref.at[area], gone.at[half, part])

    for half in range(2):
        loads[2 * half].wait()
        loads[2 * half + 1].wait()
        for part in range(4):
            for block in range(4 * part, 4 * part + 4):
                for y in range(4):
                    unit, column = block - windows[half, y], (y + 4 * half) * 128
                    if not 0 <= unit < 12:
                        continue
                    for x in range(4):
                        row = block * 64 + x * 16
                        at = (half, 0, y, x) if unit < 6 else (half, 1, x, y)
                        dense[row : row + 16, column : column + 128] = held[
                            (*at, slice(unit % 6 * 16, unit % 6 * 16 + 16), slice(None))
                        ].astype(jnp.float32)
            store(half, part).start()
    for half in range(2):
        for part in range(4):
            store(half, part).wait()


def place(shares):
    anywhere = pl.BlockSpec(memory_space=pl.ANY)
    return pl.pallas_call(
        place_kernel,
        out_shape=jax.ShapeDtypeStruct((1024, 1024), jnp.float32),
        in_specs=[anywhere],
        out_specs=anywhere,
        scratch_shapes=[
            pltpu.VMEM((2, 2, 4, 4, 96, 128), jnp.bfloat16),
            pltpu.VMEM((1024, 1024), jnp.float32),
            pltpu.SemaphoreType.DMA((4,)),
            pltpu.SemaphoreType.DMA((2, 4)),
        ],
        compiler_params=pltpu.CompilerParams(vmem_limit_bytes=61 * 2**20),
        name="place",
    )(shares)


def on_device(operator_blocks, prolong_blocks, operator_cols, coarse_map, live_rows):
    shares = fused(live_rows, operator_cols[0, 0].T, coarse_map.T, prolong_blocks[0, 0], operator_blocks[0, 0])
    return place(shares)


def solution(mesh):
    return jax.shard_map(
        on_device,
        mesh=mesh,
        in_specs=(
            P("axial", "cross", None, None, None, None),
            P("axial", "cross", None, None, None),
            P("axial", "cross", None, None),
            P(),
            P("axial", "cross"),
        ),
        out_specs=P(),
        check_vma=False,
    )
```

```python
import jax
import jax.numpy as jnp
from jax import lax
from jax.experimental import pallas as pl
from jax.experimental.pallas import tpu as pltpu
from jax.sharding import PartitionSpec as P

NCB = 16
W = 5
ROWS = 64
PIECES = ((0, 32), (32, 48), (48, 64))
CHUNKS = len(PIECES)
UNROLL = 32
MESH = pl.DeviceIdType.MESH
EMPTY = 4 * ROWS


def lowest_of(segment):
    return jnp.clip(segment - 1, 0, NCB - W)


def base_of(segment):
    low = lowest_of(jnp.maximum(segment - 1, 0))
    return jnp.minimum(low - low % 2, 8)


def fused_kernel(
    live, cols_ref, map_ref, p_ref, a_ref, shares_out,
    maps, tab, own, near, far, blocks, beside, tiles, wide, left, turned, partial, partial2, product, total, gathered,
    chunks, from_cross, from_axial, ready, units,
    tab_s, load, sent0, got0, sent1, got1, sent2, got2, sent3, got3, sent4, got4, sent5, got5, sent6, got6, flush,
):
    seg = lax.axis_index("axial")
    sec = lax.axis_index("cross")
    core = lax.rem(seg, 2)
    layer = seg // 2
    x = sec // 4
    y = lax.rem(sec, 4)
    sibling = seg + 1 - 2 * core
    beyond = seg - 1 + 2 * core
    has_far = (beyond >= 0) & (beyond < 16)
    beyond = jnp.clip(beyond, 0, 15)
    lane_off = lax.rem(sec, 2) * 64

    def remote(src, dst, send, recv, to):
        return pltpu.make_async_remote_copy(
            src_ref=src, dst_ref=dst, send_sem=send, recv_sem=recv, device_id=to, device_id_type=MESH
        )

    barrier = pltpu.get_barrier_semaphore()
    for d in range(1, 16):
        pl.semaphore_signal(barrier, inc=1, device_id=(lax.rem(seg + d, 16), sec), device_id_type=MESH)
        pl.semaphore_signal(barrier, inc=1, device_id=(seg, lax.rem(sec + d, 16)), device_id_type=MESH)

    def piece(ref, c):
        return ref.at[:, pl.ds(PIECES[c][0], PIECES[c][1] - PIECES[c][0]), :]

    own_loads = [pltpu.make_async_copy(piece(p_ref, c), piece(own, c), load.at[c]) for c in range(CHUNKS)]
    for copy in own_loads:
        copy.start()
    map_loads = []
    for part, near_seg in enumerate((seg, sibling, beyond)):
        start = pl.multiple_of((near_seg * 16 + sec - lax.rem(sec, 2)) * ROWS, 128)
        map_loads.append(pltpu.make_async_copy(map_ref.at[:, pl.ds(start, 128)], maps.at[part], load.at[CHUNKS + part]))
        map_loads[part].start()

    def block_load(c):
        return pltpu.make_async_copy(a_ref.at[pl.ds(16 * c, 16)], blocks.at[c % 2], load.at[CHUNKS + 3 + c])

    for c in range(2):
        block_load(c).start()

    def near_copy():
        return remote(own, near, sent0.at[CHUNKS], got0.at[CHUNKS], (sibling, sec))

    def far_copy(c):
        return remote(piece(own, c), piece(far, c), sent0.at[c], got0.at[c], (beyond, sec))

    in_use = live[0, 0]
    for c, (lo, hi) in enumerate(PIECES):
        own_loads[c].wait()

        @pl.loop(0, ROWS, unroll=8)
        def _(row, lo=lo, hi=hi):
            own[row, lo:hi, :] = jnp.where(row < in_use, own[row, lo:hi, :], jnp.zeros((hi - lo, 256), jnp.bfloat16))

        if c == 0:
            pl.semaphore_wait(barrier, 30)

        @pl.when(has_far)
        def _(c=c):
            far_copy(c).start()

    near_copy().start()

    slot = lax.broadcasted_iota(jnp.int32, (8, 128), 0)
    local = lax.broadcasted_iota(jnp.int32, (8, 128), 1) - lane_off
    odd = lax.rem(slot, 2)

    def find(labels, first):
        found = jnp.full((8, 128), EMPTY, jnp.int32)
        for b in range(4):
            even_tile, odd_tile = (0, 2, 1, 3)[b], (2, 0, 3, 1)[b]
            tile = even_tile + odd * (odd_tile - even_tile)
            found = jnp.where(labels[b : b + 1, :] - first == slot, 4 * local + tile, found)
        return found

    base = base_of(seg)
    for part in range(3):
        map_loads[part].wait()
        labels = maps[part]
        tab[part] = find(labels, base)
        if part == 0:
            tab[3] = find(labels, lowest_of(seg))
    named = cols_ref[...]
    named_seg = lax.shift_right_logical(named, 10)
    part = jnp.where(named_seg == seg, 0, jnp.where(named_seg == sibling, 1, 2))
    tab[4, :, 0:64] = part * ROWS + (named & 63)
    tab[4, :, 64:128] = jnp.zeros((8, 64), jnp.int32)
    to_smem = pltpu.make_async_copy(tab, tab_s, load.at[CHUNKS + 7])
    to_smem.start()

    lane_low = lax.broadcasted_iota(jnp.int32, (64, 128), 1) < 64
    tiles[EMPTY] = jnp.zeros((64, 128), jnp.bfloat16)

    def half_tiles(which, row, pair, lo, hi):
        return jnp.where(
            lane_low[lo:hi, :],
            tiles[tab_s[which, 2 * pair, lane_off + row], lo:hi, :],
            tiles[tab_s[which, 2 * pair + 1, lane_off + row], lo:hi, :],
        )

    def store_tiles(source, lo, hi):
        @pl.loop(0, ROWS, unroll=8)
        def _(row):
            value = source[row, lo:hi, :]
            for pair in range(2):
                tile = value[:, 128 * pair : 128 * pair + 128]
                tiles[4 * row + pair, lo:hi, :] = tile
                tiles[4 * row + 2 + pair, lo:hi, :] = jnp.concatenate([tile[:, 64:], tile[:, :64]], axis=1)

    def widen(part, lo, hi):
        @pl.loop(0, ROWS, unroll=8)
        def _(row):
            for pair in range(4):
                wide[part * ROWS + row, lo:hi, 128 * pair : 128 * pair + 128] = half_tiles(part, row, pair, lo, hi)

    store_tiles(own, 0, 64)
    to_smem.wait()
    widen(0, 0, 64)

    @pl.loop(0, 8)
    def _(group):
        for inner in range(8):
            for pair in range(3):
                left[64 * inner : 64 * inner + 64, 128 * pair : 128 * pair + 128] = half_tiles(
                    3, group * 8 + inner, pair, 0, 64
                )
        turned[group] = left[...].T[:320]

    for c in range(4):
        block_load(c).wait()

        @pl.loop(0, 16, unroll=2)
        def _(row, c=c):
            at = 0
            for lo, hi in PIECES:
                width = 8 * (hi - lo)
                beside[16 * c + row, :, at : at + width] = jnp.concatenate(
                    [blocks[c % 2, row, k][:, lo:hi] for k in range(8)], axis=1
                )
                at += width

        if c < 2:
            block_load(c + 2).start()

    near_copy().wait_recv()
    store_tiles(near, 0, 64)
    widen(1, 0, 64)

    sums = (partial, partial2)

    for c, (lo, hi) in enumerate(PIECES):

        @pl.when(has_far)
        def _(c=c, lo=lo, hi=hi):
            far_copy(c).wait_recv()
            store_tiles(far, lo, hi)
            widen(2, lo, hi)

        @pl.loop(0, ROWS, unroll=UNROLL)
        def _(row, c=c, lo=lo, hi=hi):
            rhs = jnp.concatenate([wide[tab_s[4, k, row], lo:hi, :] for k in range(8)], axis=0)
            term = jnp.dot(beside[row, :, 8 * lo : 8 * hi], rhs, preferred_element_type=jnp.float32)
            at = pl.ds(pl.multiple_of(row * 64, 64), 64)
            if c > 0:
                term = sums[c - 1][at, :] + term
            if c < CHUNKS - 1:
                sums[c][at, :] = term
            else:
                product[at, :] = term.astype(jnp.bfloat16)

    def cross_send(target):
        return remote(chunks.at[target], from_cross.at[sec], sent1.at[target], got1.at[sec], (seg, target))

    for half in range(2):
        columns = slice(256 * half, 256 * half + 256)
        value = None
        for group in range(8):
            term = jnp.dot(
                turned[group], product[512 * group : 512 * group + 512, columns], preferred_element_type=jnp.float32
            )
            value = term if value is None else value + term
        total[...] = value

        for quarter in range(4):
            for pair in range(2):
                target = quarter * 4 + lax.rem(base // 2 + 2 * half + pair, 4)
                for block in range(W):
                    at = block * 64 + quarter * 16
                    chunks[target, block * 16 : block * 16 + 16, :] = total[
                        at : at + 16, 128 * pair : 128 * pair + 128
                    ].astype(jnp.bfloat16)

                @pl.when(target != sec)
                def _(target=target):
                    cross_send(target).start()

    value = chunks[sec].astype(jnp.float32)
    for d in range(1, 16):
        source = lax.rem(sec + d, 16)
        remote(chunks.at[source], from_cross.at[source], sent1.at[source], got1.at[source], (seg, source)).wait_recv()
        value = value + from_cross[source].astype(jnp.float32)
    units[0:80, :] = value
    units[80:112, :] = jnp.zeros((32, 128), jnp.float32)

    def half_of(segment):
        start = base_of(segment) // 2
        return (start + lax.rem(y - start + 8, 4)) // 4

    my_half = half_of(seg)
    my_low = lowest_of(seg)

    def axial_copy(i):
        block = my_low + i
        owner = (block // 2) * 2 + my_half
        place = lax.rem(block, 2)
        copy = remote(
            units.at[pl.ds(16 * i, 16)], from_axial.at[seg, place], sent2.at[i], got2.at[seg, place], (owner, sec)
        )
        return owner, place, copy

    for i in range(W):
        owner, place, copy = axial_copy(i)

        @pl.when(owner != seg)
        def _(copy=copy):
            copy.start()

        @pl.when(owner == seg)
        def _(i=i, place=place):
            from_axial[seg, place] = units[16 * i : 16 * i + 16, :]

    first_source = jnp.where(2 * layer <= 4, 0, 2 * layer - 3)
    end_source = jnp.where(2 * layer + 1 >= NCB - W, 16, 2 * layer + 3)

    @pl.loop(first_source, end_source)
    def _(source):
        low = lowest_of(source)
        for place in range(2):
            block = 2 * layer + place

            @pl.when((half_of(source) == core) & (block >= low) & (block < low + W))
            def _(place=place):
                @pl.when(source != seg)
                def _():
                    remote(
                        units.at[pl.ds(0, 16)],
                        from_axial.at[source, place],
                        sent2.at[0],
                        got2.at[source, place],
                        (sibling, sec),
                    ).wait_recv()

                units[80 + 16 * place : 96 + 16 * place, :] += from_axial[source, place]

    mine = pl.ds(pl.multiple_of(layer * 32, 32), 32)
    ready[mine, :] = units[80:112, :].astype(jnp.bfloat16)

    def layer_copy(d):
        return remote(ready.at[mine], ready.at[mine], sent3.at[d], got3.at[d], (lax.rem(seg + 2 * d, 16), sec))

    for d in range(1, 8):
        layer_copy(d).start()
    for d in range(1, 8):
        source = pl.ds(pl.multiple_of(lax.rem(layer - d + 8, 8) * 32, 32), 32)
        remote(ready.at[source], ready.at[source], sent3.at[d], got3.at[d], (sibling, sec)).wait_recv()

    first = jnp.where(core == 0, y // 3, jnp.minimum(3 + y, 4))
    gathered[0, y, x] = ready[pl.ds(pl.multiple_of(first * 16, 16), 96), :]
    gathered[1, x, y] = ready[pl.ds(pl.multiple_of(first * 16 + 96, 16), 96), :]

    def moved(which, d):
        return (seg, lax.rem(x + d, 4) * 4 + y) if which == 0 else (seg, x * 4 + lax.rem(y + d, 4))

    def back(which, d):
        return lax.rem((x if which == 0 else y) - d + 4, 4)

    def one_copy(which, d):
        major, minor = (y, x) if which == 0 else (x, y)
        share = gathered.at[which, major, minor]
        return remote(share, share, sent4.at[which, d], got4.at[which, d], moved(which, d))

    def next_copy(which, d, j):
        share = gathered.at[which, y if which == 0 else x, back(which, j)]
        return remote(share, share, sent5.at[which, d, j], got5.at[which, d, j], moved(1 - which, d))

    def pass_copy(half, which, d):
        place = back(1 - which, d)
        shares = gathered.at[which, place]
        return remote(shares, shares_out.at[half, which, place], sent6.at[which, d], got6.at[which, d], (sibling, sec))

    def keep_copy(which, d):
        place = back(1 - which, d)
        return pltpu.make_async_copy(gathered.at[which, place], shares_out.at[core, which, place], flush.at[which, d])

    for d in (2, 1, 3):
        for which in range(2):
            one_copy(which, d).start()
    for d in (2, 1, 3):
        for which in range(2):
            next_copy(which, d, 0).start()
    for j in (1, 3, 2):
        for which in range(2):
            share = gathered.at[which, y if which == 0 else x, back(which, j)]
            remote(share, share, sent4.at[which, j], got4.at[which, j], (sibling, sec)).wait_recv()
            for d in (2, 1, 3):
                next_copy(which, d, j).start()
    for which in range(2):
        pass_copy(core, which, 0).start()
        keep_copy(which, 0).start()
    for d in (1, 3, 2):
        for which in range(2):
            for j in (0, 1, 3, 2):
                share = gathered.at[which, back(1 - which, d), back(which, j)]
                remote(share, share, sent5.at[which, d, j], got5.at[which, d, j], (sibling, sec)).wait_recv()
            pass_copy(core, which, d).start()
            keep_copy(which, d).start()
    for which in range(2):
        for d in range(4):
            pass_copy(1 - core, which, d).wait_recv()

    near_copy().wait_send()
    for c in range(CHUNKS):

        @pl.when(has_far)
        def _(c=c):
            far_copy(c).wait_send()

    for d in range(1, 16):
        cross_send(lax.rem(sec + d, 16)).wait_send()
    for i in range(W):
        owner, _, copy = axial_copy(i)

        @pl.when(owner != seg)
        def _(copy=copy):
            copy.wait_send()

    for d in range(1, 8):
        layer_copy(d).wait_send()
    for which in range(2):
        for d in range(1, 4):
            one_copy(which, d).wait_send()
            for j in range(4):
                next_copy(which, d, j).wait_send()
        for d in range(4):
            pass_copy(core, which, d).wait_send()
            keep_copy(which, d).wait()


def fused(live, cols, coarse, prolong, operator):
    dma = pltpu.SemaphoreType.DMA
    vmem = pl.BlockSpec(memory_space=pltpu.VMEM)
    anywhere = pl.BlockSpec(memory_space=pl.ANY)
    bf16, f32, i32 = jnp.bfloat16, jnp.float32, jnp.int32
    return pl.pallas_call(
        fused_kernel,
        out_shape=jax.ShapeDtypeStruct((2, 2, 4, 4, 96, 128), bf16),
        in_specs=[pl.BlockSpec(memory_space=pltpu.SMEM), vmem, anywhere, anywhere, anywhere],
        out_specs=anywhere,
        scratch_shapes=[
            pltpu.VMEM((3, 4, 128), i32),
            pltpu.VMEM((5, 8, 128), i32),
            pltpu.VMEM((ROWS, 64, 256), bf16),
            pltpu.VMEM((ROWS, 64, 256), bf16),
            pltpu.VMEM((ROWS, 64, 256), bf16),
            pltpu.VMEM((2, 16, 8, 64, 64), bf16),
            pltpu.VMEM((ROWS, 64, 512), bf16),
            pltpu.VMEM((4 * ROWS + 1, 64, 128), bf16),
            pltpu.VMEM((3 * ROWS, 64, 512), bf16),
            pltpu.VMEM((512, 384), bf16),
            pltpu.VMEM((8, 320, 512), bf16),
            pltpu.VMEM((ROWS * 64, 512), f32),
            pltpu.VMEM((ROWS * 64, 512), f32),
            pltpu.VMEM((ROWS * 64, 512), bf16),
            pltpu.VMEM((320, 256), f32),
            pltpu.VMEM((2, 4, 4, 96, 128), bf16),
            pltpu.VMEM((16, 80, 128), bf16),
            pltpu.VMEM((16, 80, 128), bf16),
            pltpu.VMEM((16, 2, 16, 128), f32),
            pltpu.VMEM((256, 128), bf16),
            pltpu.VMEM((112, 128), f32),
            pltpu.SMEM((5, 8, 128), i32),
            dma((CHUNKS + 8,)),
            dma((CHUNKS + 1,)),
            dma((CHUNKS + 1,)),
            dma((16,)),
            dma((16,)),
            dma((W,)),
            dma((16, 2)),
            dma((8,)),
            dma((8,)),
            dma((2, 4)),
            dma((2, 4)),
            dma((2, 4, 4)),
            dma((2, 4, 4)),
            dma((2, 4)),
            dma((2, 4)),
            dma((2, 4)),
        ],
        compiler_params=pltpu.CompilerParams(collective_id=0, has_side_effects=True, vmem_limit_bytes=61 * 2**20),
        name="fused",
    )(live, cols, coarse, prolong, operator)


def place_kernel(shares, out_ref, held, dense, got, gone):
    loads = [pltpu.make_async_copy(shares.at[i // 2, i % 2], held.at[i // 2, i % 2], got.at[i]) for i in range(4)]
    for load in loads:
        load.start()
    windows = {(half, y): y // 3 if half == 0 else min(3 + y, 4) for half in range(2) for y in range(4)}
    for (half, y), first in windows.items():
        column = (y + 4 * half) * 128
        for start, end in ((0, first * 64), ((first + 12) * 64, 1024)):
            if end > start:
                dense[start:end, column : column + 128] = jnp.zeros((end - start, 128), jnp.float32)

    def store(half, part):
        area = (pl.ds(part * 256, 256), pl.ds(half * 512, 512))
        return pltpu.make_async_copy(dense.at[area], out_ref.at[area], gone.at[half, part])

    for half in range(2):
        loads[2 * half].wait()
        loads[2 * half + 1].wait()
        for part in range(4):
            for block in range(4 * part, 4 * part + 4):
                for y in range(4):
                    unit, column = block - windows[half, y], (y + 4 * half) * 128
                    if not 0 <= unit < 12:
                        continue
                    for x in range(4):
                        row = block * 64 + x * 16
                        at = (half, 0, y, x) if unit < 6 else (half, 1, x, y)
                        dense[row : row + 16, column : column + 128] = held[
                            (*at, slice(unit % 6 * 16, unit % 6 * 16 + 16), slice(None))
                        ].astype(jnp.float32)
            store(half, part).start()
    for half in range(2):
        for part in range(4):
            store(half, part).wait()


def place(shares):
    anywhere = pl.BlockSpec(memory_space=pl.ANY)
    return pl.pallas_call(
        place_kernel,
        out_shape=jax.ShapeDtypeStruct((1024, 1024), jnp.float32),
        in_specs=[anywhere],
        out_specs=anywhere,
        scratch_shapes=[
            pltpu.VMEM((2, 2, 4, 4, 96, 128), jnp.bfloat16),
            pltpu.VMEM((1024, 1024), jnp.float32),
            pltpu.SemaphoreType.DMA((4,)),
            pltpu.SemaphoreType.DMA((2, 4)),
        ],
        compiler_params=pltpu.CompilerParams(vmem_limit_bytes=61 * 2**20),
        name="place",
    )(shares)


def on_device(operator_blocks, prolong_blocks, operator_cols, coarse_map, live_rows):
    shares = fused(live_rows, operator_cols[0, 0].T, coarse_map.T, prolong_blocks[0, 0], operator_blocks[0, 0])
    return place(shares)


def solution(mesh):
    return jax.shard_map(
        on_device,
        mesh=mesh,
        in_specs=(
            P("axial", "cross", None, None, None, None),
            P("axial", "cross", None, None, None),
            P("axial", "cross", None, None),
            P(),
            P("axial", "cross"),
        ),
        out_specs=P(),
        check_vma=False,
    )
```

```python
import jax
import jax.numpy as jnp
from jax import lax
from jax.experimental import pallas as pl
from jax.experimental.pallas import tpu as pltpu
from jax.sharding import PartitionSpec as P

NCB = 16
W = 5
ROWS = 64
PIECES = ((0, 32), (32, 48), (48, 64))
CHUNKS = len(PIECES)
PARTS = 4
UNROLL = 32
MESH = pl.DeviceIdType.MESH
EMPTY = 4 * ROWS


def lowest_of(segment):
    return jnp.clip(segment - 1, 0, NCB - W)


def base_of(segment):
    low = lowest_of(jnp.maximum(segment - 1, 0))
    return jnp.minimum(low - low % 2, 8)


def fused_kernel(
    live, cols_ref, map_ref, p_ref, a_ref, shares_out,
    maps, tab, own, near, far, blocks, beside, tiles, wide, left, turned, partial, partial2, product, total, gathered,
    chunks, from_cross, from_axial, ready, units,
    tab_s, load, sent0, got0, sent1, got1, sent2, got2, sent3, got3, sent4, got4, sent5, got5, sent6, got6, flush,
):
    seg = lax.axis_index("axial")
    sec = lax.axis_index("cross")
    core = lax.rem(seg, 2)
    layer = seg // 2
    x = sec // 4
    y = lax.rem(sec, 4)
    sibling = seg + 1 - 2 * core
    beyond = seg - 1 + 2 * core
    has_far = (beyond >= 0) & (beyond < 16)
    beyond = jnp.clip(beyond, 0, 15)
    lane_off = lax.rem(sec, 2) * 64

    def remote(src, dst, send, recv, to):
        return pltpu.make_async_remote_copy(
            src_ref=src, dst_ref=dst, send_sem=send, recv_sem=recv, device_id=to, device_id_type=MESH
        )

    def part_of(ref, c):
        return ref.at[:, pl.ds(16 * c, 16), :]

    own_loads = [pltpu.make_async_copy(part_of(p_ref, c), part_of(own, c), load.at[c]) for c in range(PARTS)]
    own_loads[0].start()
    barrier = pltpu.get_barrier_semaphore()
    pl.semaphore_signal(barrier, inc=1, device_id=(lax.rem(seg + 1, 16), sec), device_id_type=MESH)
    pl.semaphore_signal(barrier, inc=1, device_id=(lax.rem(seg + 15, 16), sec), device_id_type=MESH)
    for copy in own_loads[1:]:
        copy.start()
    for d in range(1, 16):
        if 1 < d < 15:
            pl.semaphore_signal(barrier, inc=1, device_id=(lax.rem(seg + d, 16), sec), device_id_type=MESH)
        pl.semaphore_signal(barrier, inc=1, device_id=(seg, lax.rem(sec + d, 16)), device_id_type=MESH)

    map_loads = []
    for part, near_seg in enumerate((seg, sibling, beyond)):
        start = pl.multiple_of((near_seg * 16 + sec - lax.rem(sec, 2)) * ROWS, 128)
        map_loads.append(pltpu.make_async_copy(map_ref.at[:, pl.ds(start, 128)], maps.at[part], load.at[PARTS + part]))
        map_loads[part].start()

    def block_load(c):
        return pltpu.make_async_copy(a_ref.at[pl.ds(16 * c, 16)], blocks.at[c % 2], load.at[PARTS + 3 + c])

    for c in range(2):
        block_load(c).start()

    def near_copy():
        return remote(own, near, sent0.at[PARTS], got0.at[PARTS], (sibling, sec))

    def far_copy(c):
        return remote(part_of(own, c), part_of(far, c), sent0.at[c], got0.at[c], (beyond, sec))

    in_use = live[0, 0]
    for c in range(PARTS):
        own_loads[c].wait()

        @pl.loop(0, ROWS, unroll=8)
        def _(row, rows=slice(16 * c, 16 * c + 16)):
            own[row, rows, :] = jnp.where(row < in_use, own[row, rows, :], jnp.zeros((16, 256), jnp.bfloat16))

        if c == 0:
            pl.semaphore_wait(barrier, 30)

        @pl.when(has_far)
        def _(c=c):
            far_copy(c).start()

    near_copy().start()

    slot = lax.broadcasted_iota(jnp.int32, (8, 128), 0)
    local = lax.broadcasted_iota(jnp.int32, (8, 128), 1) - lane_off
    odd = lax.rem(slot, 2)

    def find(labels, first):
        found = jnp.full((8, 128), EMPTY, jnp.int32)
        for b in range(4):
            even_tile, odd_tile = (0, 2, 1, 3)[b], (2, 0, 3, 1)[b]
            tile = even_tile + odd * (odd_tile - even_tile)
            found = jnp.where(labels[b : b + 1, :] - first == slot, 4 * local + tile, found)
        return found

    base = base_of(seg)
    for part in range(3):
        map_loads[part].wait()
        labels = maps[part]
        tab[part] = find(labels, base)
        if part == 0:
            tab[3] = find(labels, lowest_of(seg))
    named = cols_ref[...]
    named_seg = lax.shift_right_logical(named, 10)
    part = jnp.where(named_seg == seg, 0, jnp.where(named_seg == sibling, 1, 2))
    tab[4, :, 0:64] = part * ROWS + (named & 63)
    tab[4, :, 64:128] = jnp.zeros((8, 64), jnp.int32)
    to_smem = pltpu.make_async_copy(tab, tab_s, load.at[PARTS + 7])
    to_smem.start()

    lane_low = lax.broadcasted_iota(jnp.int32, (64, 128), 1) < 64
    tiles[EMPTY] = jnp.zeros((64, 128), jnp.bfloat16)

    def half_tiles(which, row, pair, lo, hi):
        return jnp.where(
            lane_low[lo:hi, :],
            tiles[tab_s[which, 2 * pair, lane_off + row], lo:hi, :],
            tiles[tab_s[which, 2 * pair + 1, lane_off + row], lo:hi, :],
        )

    def store_tiles(source, lo, hi):
        @pl.loop(0, ROWS, unroll=8)
        def _(row):
            value = source[row, lo:hi, :]
            for pair in range(2):
                tile = value[:, 128 * pair : 128 * pair + 128]
                tiles[4 * row + pair, lo:hi, :] = tile
                tiles[4 * row + 2 + pair, lo:hi, :] = jnp.concatenate([tile[:, 64:], tile[:, :64]], axis=1)

    def widen(part, lo, hi):
        @pl.loop(0, ROWS, unroll=8)
        def _(row):
            for pair in range(4):
                wide[part * ROWS + row, lo:hi, 128 * pair : 128 * pair + 128] = half_tiles(part, row, pair, lo, hi)

    store_tiles(own, 0, 64)
    to_smem.wait()
    widen(0, 0, 64)

    @pl.loop(0, 8)
    def _(group):
        for inner in range(8):
            for pair in range(3):
                left[64 * inner : 64 * inner + 64, 128 * pair : 128 * pair + 128] = half_tiles(
                    3, group * 8 + inner, pair, 0, 64
                )
        turned[group] = left[...].T[:320]

    for c in range(4):
        block_load(c).wait()

        @pl.loop(0, 16, unroll=2)
        def _(row, c=c):
            at = 0
            for lo, hi in PIECES:
                width = 8 * (hi - lo)
                beside[16 * c + row, :, at : at + width] = jnp.concatenate(
                    [blocks[c % 2, row, k][:, lo:hi] for k in range(8)], axis=1
                )
                at += width

        if c < 2:
            block_load(c + 2).start()

    near_copy().wait_recv()
    store_tiles(near, 0, 64)
    widen(1, 0, 64)

    sums = (partial, partial2)

    for c, (lo, hi) in enumerate(PIECES):

        @pl.when(has_far)
        def _(c=c, lo=lo, hi=hi):
            for part in range(lo // 16, hi // 16):
                far_copy(part).wait_recv()
            store_tiles(far, lo, hi)
            widen(2, lo, hi)

        @pl.loop(0, ROWS, unroll=UNROLL)
        def _(row, c=c, lo=lo, hi=hi):
            rhs = jnp.concatenate([wide[tab_s[4, k, row], lo:hi, :] for k in range(8)], axis=0)
            term = jnp.dot(beside[row, :, 8 * lo : 8 * hi], rhs, preferred_element_type=jnp.float32)
            at = pl.ds(pl.multiple_of(row * 64, 64), 64)
            if c > 0:
                term = sums[c - 1][at, :] + term
            if c < CHUNKS - 1:
                sums[c][at, :] = term
            else:
                product[at, :] = term.astype(jnp.bfloat16)

    def cross_send(target):
        return remote(chunks.at[target], from_cross.at[sec], sent1.at[target], got1.at[sec], (seg, target))

    for half in range(2):
        columns = slice(256 * half, 256 * half + 256)
        value = None
        for group in range(8):
            term = jnp.dot(
                turned[group], product[512 * group : 512 * group + 512, columns], preferred_element_type=jnp.float32
            )
            value = term if value is None else value + term
        total[...] = value

        for quarter in range(4):
            for pair in range(2):
                target = quarter * 4 + lax.rem(base // 2 + 2 * half + pair, 4)
                for block in range(W):
                    at = block * 64 + quarter * 16
                    chunks[target, block * 16 : block * 16 + 16, :] = total[
                        at : at + 16, 128 * pair : 128 * pair + 128
                    ].astype(jnp.bfloat16)

                @pl.when(target != sec)
                def _(target=target):
                    cross_send(target).start()

    value = chunks[sec].astype(jnp.float32)
    for d in range(1, 16):
        source = lax.rem(sec + d, 16)
        remote(chunks.at[source], from_cross.at[source], sent1.at[source], got1.at[source], (seg, source)).wait_recv()
        value = value + from_cross[source].astype(jnp.float32)
    units[0:80, :] = value
    units[80:112, :] = jnp.zeros((32, 128), jnp.float32)

    def half_of(segment):
        start = base_of(segment) // 2
        return (start + lax.rem(y - start + 8, 4)) // 4

    my_half = half_of(seg)
    my_low = lowest_of(seg)

    def axial_copy(i):
        block = my_low + i
        owner = (block // 2) * 2 + my_half
        place = lax.rem(block, 2)
        copy = remote(
            units.at[pl.ds(16 * i, 16)], from_axial.at[seg, place], sent2.at[i], got2.at[seg, place], (owner, sec)
        )
        return owner, place, copy

    for i in range(W):
        owner, place, copy = axial_copy(i)

        @pl.when(owner != seg)
        def _(copy=copy):
            copy.start()

        @pl.when(owner == seg)
        def _(i=i, place=place):
            from_axial[seg, place] = units[16 * i : 16 * i + 16, :]

    first_source = jnp.where(2 * layer <= 4, 0, 2 * layer - 3)
    end_source = jnp.where(2 * layer + 1 >= NCB - W, 16, 2 * layer + 3)

    @pl.loop(first_source, end_source)
    def _(source):
        low = lowest_of(source)
        for place in range(2):
            block = 2 * layer + place

            @pl.when((half_of(source) == core) & (block >= low) & (block < low + W))
            def _(place=place):
                @pl.when(source != seg)
                def _():
                    remote(
                        units.at[pl.ds(0, 16)],
                        from_axial.at[source, place],
                        sent2.at[0],
                        got2.at[source, place],
                        (sibling, sec),
                    ).wait_recv()

                units[80 + 16 * place : 96 + 16 * place, :] += from_axial[source, place]

    mine = pl.ds(pl.multiple_of(layer * 32, 32), 32)
    ready[mine, :] = units[80:112, :].astype(jnp.bfloat16)

    def layer_copy(d):
        return remote(ready.at[mine], ready.at[mine], sent3.at[d], got3.at[d], (lax.rem(seg + 2 * d, 16), sec))

    for d in range(1, 8):
        layer_copy(d).start()
    for d in range(1, 8):
        source = pl.ds(pl.multiple_of(lax.rem(layer - d + 8, 8) * 32, 32), 32)
        remote(ready.at[source], ready.at[source], sent3.at[d], got3.at[d], (sibling, sec)).wait_recv()

    first = jnp.where(core == 0, y // 3, jnp.minimum(3 + y, 4))
    gathered[0, y, x] = ready[pl.ds(pl.multiple_of(first * 16, 16), 96), :]
    gathered[1, x, y] = ready[pl.ds(pl.multiple_of(first * 16 + 96, 16), 96), :]

    def moved(which, d):
        return (seg, lax.rem(x + d, 4) * 4 + y) if which == 0 else (seg, x * 4 + lax.rem(y + d, 4))

    def back(which, d):
        return lax.rem((x if which == 0 else y) - d + 4, 4)

    def one_copy(which, d):
        major, minor = (y, x) if which == 0 else (x, y)
        share = gathered.at[which, major, minor]
        return remote(share, share, sent4.at[which, d], got4.at[which, d], moved(which, d))

    def next_copy(which, d, j):
        share = gathered.at[which, y if which == 0 else x, back(which, j)]
        return remote(share, share, sent5.at[which, d, j], got5.at[which, d, j], moved(1 - which, d))

    def pass_copy(half, which, d):
        place = back(1 - which, d)
        shares = gathered.at[which, place]
        return remote(shares, shares_out.at[half, which, place], sent6.at[which, d], got6.at[which, d], (sibling, sec))

    def keep_copy(which, d):
        place = back(1 - which, d)
        return pltpu.make_async_copy(gathered.at[which, place], shares_out.at[core, which, place], flush.at[which, d])

    for d in (2, 1, 3):
        for which in range(2):
            one_copy(which, d).start()
    for d in (2, 1, 3):
        for which in range(2):
            next_copy(which, d, 0).start()
    for j in (1, 3, 2):
        for which in range(2):
            share = gathered.at[which, y if which == 0 else x, back(which, j)]
            remote(share, share, sent4.at[which, j], got4.at[which, j], (sibling, sec)).wait_recv()
            for d in (2, 1, 3):
                next_copy(which, d, j).start()
    for which in range(2):
        pass_copy(core, which, 0).start()
        keep_copy(which, 0).start()
    for d in (1, 3, 2):
        for which in range(2):
            for j in (0, 1, 3, 2):
                share = gathered.at[which, back(1 - which, d), back(which, j)]
                remote(share, share, sent5.at[which, d, j], got5.at[which, d, j], (sibling, sec)).wait_recv()
            pass_copy(core, which, d).start()
            keep_copy(which, d).start()
    for which in range(2):
        for d in range(4):
            pass_copy(1 - core, which, d).wait_recv()

    near_copy().wait_send()
    for c in range(PARTS):

        @pl.when(has_far)
        def _(c=c):
            far_copy(c).wait_send()

    for d in range(1, 16):
        cross_send(lax.rem(sec + d, 16)).wait_send()
    for i in range(W):
        owner, _, copy = axial_copy(i)

        @pl.when(owner != seg)
        def _(copy=copy):
            copy.wait_send()

    for d in range(1, 8):
        layer_copy(d).wait_send()
    for which in range(2):
        for d in range(1, 4):
            one_copy(which, d).wait_send()
            for j in range(4):
                next_copy(which, d, j).wait_send()
        for d in range(4):
            pass_copy(core, which, d).wait_send()
            keep_copy(which, d).wait()


def fused(live, cols, coarse, prolong, operator):
    dma = pltpu.SemaphoreType.DMA
    vmem = pl.BlockSpec(memory_space=pltpu.VMEM)
    anywhere = pl.BlockSpec(memory_space=pl.ANY)
    bf16, f32, i32 = jnp.bfloat16, jnp.float32, jnp.int32
    return pl.pallas_call(
        fused_kernel,
        out_shape=jax.ShapeDtypeStruct((2, 2, 4, 4, 96, 128), bf16),
        in_specs=[pl.BlockSpec(memory_space=pltpu.SMEM), vmem, anywhere, anywhere, anywhere],
        out_specs=anywhere,
        scratch_shapes=[
            pltpu.VMEM((3, 4, 128), i32),
            pltpu.VMEM((5, 8, 128), i32),
            pltpu.VMEM((ROWS, 64, 256), bf16),
            pltpu.VMEM((ROWS, 64, 256), bf16),
            pltpu.VMEM((ROWS, 64, 256), bf16),
            pltpu.VMEM((2, 16, 8, 64, 64), bf16),
            pltpu.VMEM((ROWS, 64, 512), bf16),
            pltpu.VMEM((4 * ROWS + 1, 64, 128), bf16),
            pltpu.VMEM((3 * ROWS, 64, 512), bf16),
            pltpu.VMEM((512, 384), bf16),
            pltpu.VMEM((8, 320, 512), bf16),
            pltpu.VMEM((ROWS * 64, 512), f32),
            pltpu.VMEM((ROWS * 64, 512), f32),
            pltpu.VMEM((ROWS * 64, 512), bf16),
            pltpu.VMEM((320, 256), f32),
            pltpu.VMEM((2, 4, 4, 96, 128), bf16),
            pltpu.VMEM((16, 80, 128), bf16),
            pltpu.VMEM((16, 80, 128), bf16),
            pltpu.VMEM((16, 2, 16, 128), f32),
            pltpu.VMEM((256, 128), bf16),
            pltpu.VMEM((112, 128), f32),
            pltpu.SMEM((5, 8, 128), i32),
            dma((PARTS + 8,)),
            dma((PARTS + 1,)),
            dma((PARTS + 1,)),
            dma((16,)),
            dma((16,)),
            dma((W,)),
            dma((16, 2)),
            dma((8,)),
            dma((8,)),
            dma((2, 4)),
            dma((2, 4)),
            dma((2, 4, 4)),
            dma((2, 4, 4)),
            dma((2, 4)),
            dma((2, 4)),
            dma((2, 4)),
        ],
        compiler_params=pltpu.CompilerParams(collective_id=0, has_side_effects=True, vmem_limit_bytes=61 * 2**20),
        name="fused",
    )(live, cols, coarse, prolong, operator)


def place_kernel(shares, out_ref, held, dense, got, gone):
    loads = [pltpu.make_async_copy(shares.at[i // 2, i % 2], held.at[i // 2, i % 2], got.at[i]) for i in range(4)]
    for load in loads:
        load.start()
    windows = {(half, y): y // 3 if half == 0 else min(3 + y, 4) for half in range(2) for y in range(4)}
    for (half, y), first in windows.items():
        column = (y + 4 * half) * 128
        for start, end in ((0, first * 64), ((first + 12) * 64, 1024)):
            if end > start:
                dense[start:end, column : column + 128] = jnp.zeros((end - start, 128), jnp.float32)

    def store(half, part):
        area = (pl.ds(part * 256, 256), pl.ds(half * 512, 512))
        return pltpu.make_async_copy(dense.at[area], out_ref.at[area], gone.at[half, part])

    for half in range(2):
        loads[2 * half].wait()
        loads[2 * half + 1].wait()
        for part in range(4):
            for block in range(4 * part, 4 * part + 4):
                for y in range(4):
                    unit, column = block - windows[half, y], (y + 4 * half) * 128
                    if not 0 <= unit < 12:
                        continue
                    for x in range(4):
                        row = block * 64 + x * 16
                        at = (half, 0, y, x) if unit < 6 else (half, 1, x, y)
                        dense[row : row + 16, column : column + 128] = held[
                            (*at, slice(unit % 6 * 16, unit % 6 * 16 + 16), slice(None))
                        ].astype(jnp.float32)
            store(half, part).start()
    for half in range(2):
        for part in range(4):
            store(half, part).wait()


def place(shares):
    anywhere = pl.BlockSpec(memory_space=pl.ANY)
    return pl.pallas_call(
        place_kernel,
        out_shape=jax.ShapeDtypeStruct((1024, 1024), jnp.float32),
        in_specs=[anywhere],
        out_specs=anywhere,
        scratch_shapes=[
            pltpu.VMEM((2, 2, 4, 4, 96, 128), jnp.bfloat16),
            pltpu.VMEM((1024, 1024), jnp.float32),
            pltpu.SemaphoreType.DMA((4,)),
            pltpu.SemaphoreType.DMA((2, 4)),
        ],
        compiler_params=pltpu.CompilerParams(vmem_limit_bytes=61 * 2**20),
        name="place",
    )(shares)


def on_device(operator_blocks, prolong_blocks, operator_cols, coarse_map, live_rows):
    shares = fused(live_rows, operator_cols[0, 0].T, coarse_map.T, prolong_blocks[0, 0], operator_blocks[0, 0])
    return place(shares)


def solution(mesh):
    return jax.shard_map(
        on_device,
        mesh=mesh,
        in_specs=(
            P("axial", "cross", None, None, None, None),
            P("axial", "cross", None, None, None),
            P("axial", "cross", None, None),
            P(),
            P("axial", "cross"),
        ),
        out_specs=P(),
        check_vma=False,
    )
```
